32 devices in a mesh: row: 4 (over y, core), col: 8 (over z, x).
Axes of the slice: x: 2, y: 2, z: 4, core: 2. Of those that a mesh axis runs over, the one named last changes fastest.
Arguments:
- reversed_rows: float32 [4, 4, 256, 2, 8, 256], P(None, 'row', None, None, 'col'), may hold values from -0.375 to 0.375
- state: float32 [4, 4, 256, 2, 8, 256], P(None, 'row', None, None, 'col'), may hold values from -6 to 6
- basis: float32 [4, 4, 256, 256], P(None, 'row'), may hold values from -1 to 2
- eigval: float32 [4, 4, 256], P(None, 'row'), may hold values from -4 to -0.5
Outputs:
- updated: float32 [4, 4, 256, 2, 8, 256], P(None, 'row', None, None, 'col')
The draws below stay inside these ranges and needn't reach their ends.
All inputs are finite; a program needn't handle non-finite values.
Results may differ from the reference program's by a relative error of at most 0.00013.
Values sent between devices are 32-bit elements; how exact they have to be, the bound alone decides.
No kernel may reach another device: no remote copies, remote signals or barrier semaphores. Data moves between devices by JAX's collectives and lax.ppermute only.
A program may use at most 64 MiB of HBM per device.

```python
import math
import jax
import jax.numpy as jnp
from jax import lax

NB = 256
BR = 4
BC = 2
N_ROW = 4
N_COL = 8


def draw_basis(key, part):
    key = jax.random.fold_in(key, 7)
    spread = 0.5 / math.sqrt(NB)
    noise = spread * jax.random.truncated_normal(key, -3.0, 3.0, (BR, N_ROW, NB, NB), jnp.float32)
    return noise + jnp.eye(NB, dtype=jnp.float32)


def block_levels(key, shape, shards, least, high):
    gain = 1.0
    for dim, blocks in shards:
        heights = jax.random.uniform(jax.random.fold_in(jax.random.fold_in(key, 6), dim), (blocks,), jnp.float32, least / len(shards), high / len(shards))
        gain = gain * jnp.repeat(jnp.exp(heights), shape[dim] // blocks).reshape((-1,) + (1,) * (len(shape) - 1 - dim))
    return gain


def gaussian(own_key, shape, deviation, bound, cuts=(), kind=jnp.bfloat16):
    result = jax.random.normal(own_key, shape, jnp.float32) * deviation
    if len(cuts) > 0:
        result = block_levels(own_key, shape, cuts, -0.22, 0.18) * result
    return jnp.clip(result, min=-bound, max=bound).astype(kind)


def setup_inputs(seed: int = 0) -> dict:
    splits = jax.random.split(jax.random.key(seed), 5)
    return {
        "reversed_rows": gaussian(splits[0], (BR, N_ROW, NB, BC, N_COL, NB), NB ** -0.5, 0.375, ((1, 4), (4, 8)), jnp.float32),
        "state": gaussian(splits[1], (BR, N_ROW, NB, BC, N_COL, NB), 1.0, 6.0, ((1, 4), (4, 8)), jnp.float32),
        "basis": draw_basis(jax.random.fold_in(splits[4], 71), 0),
        "eigval": jnp.clip(-4.0 + 3.5 * jax.random.uniform(splits[3], (BR, N_ROW, NB), jnp.float32) ** block_levels(splits[3], (BR, N_ROW, NB), ((1, 4),), -0.2, 0.2), -4.0, -0.5),
    }


def product(first, second):
    return jnp.dot(first, second, precision=lax.Precision.HIGHEST, preferred_element_type=jnp.float32)


def reference(reversed_rows, state, basis, eigval):
    block_count = BR * N_ROW
    upper_rows = reversed_rows.reshape(block_count, NB, block_count, NB)[::-1]
    running = state.reshape(block_count, NB, block_count, NB)
    block_bases = basis.reshape(block_count, NB, NB)
    block_values = eigval.reshape(block_count, NB)
    column_ids = jnp.arange(block_count)
    placed = {}
    for diagonal in (block_count - 1, block_count):
        solved = {}
        for block_row in range(block_count):
            block_col = diagonal - block_row
            if block_row <= block_col < block_count:
                right_side = running[block_row, :, block_col, :] + running[block_col, :, block_row, :].T
                inner_part = product(product(block_bases[block_row].T, right_side), block_bases[block_col])
                inner_part = inner_part / (block_values[block_row][:, None] + block_values[block_col][None, :])
                solution = product(product(block_bases[block_row], inner_part), block_bases[block_col].T)
                solved[(block_row, block_col)] = solution
                if block_row < block_col:
                    solved[(block_col, block_row)] = solution.T
        for block_row in range(block_count):
            partner = diagonal - block_row
            if 0 <= partner < block_count:
                changes = jnp.einsum("ab,bjd->ajd", solved[(block_row, partner)], upper_rows[partner], precision=lax.Precision.HIGHEST, preferred_element_type=jnp.float32)
                column_mask = (column_ids > partner)[None, :, None]
                running = running.at[block_row].add(-jnp.where(column_mask, changes, 0.0))
        placed.update(solved)
    for position, content in placed.items():
        running = running.at[position[0], :, position[1], :].set(content)
    return running.reshape(state.shape)
```

```python
import numpy as np
import jax
import jax.numpy as jnp
from jax import lax
from jax.sharding import PartitionSpec as P

AXES = ("row", "col")
PRECISION = lax.Precision.HIGH


def product(first, second):
    return jnp.dot(first, second, precision=PRECISION, preferred_element_type=jnp.float32)


class Plan:
    def __init__(self, rows, cols, block_rows, block_cols):
        self.rows, self.cols = rows, cols
        self.count = block_rows * rows
        assert block_rows == 4 and block_cols == 2 and self.count == block_cols * cols
        self.line = 4
        self.stride = cols // self.line

    def table(self, function):
        values = [[function(r, c) for c in range(self.cols)] for r in range(self.rows)]
        return np.asarray(values)

    def own_mirror(self, r):
        return r == (-r) % self.rows

    def keys(self, r):
        return [p * self.rows + r for p in range(4)]

    def place(self, k, d):
        m = d - k
        return (k % self.rows, m % self.cols), k // self.rows, m // self.cols

    def solver_first(self, k):
        r, p = k % self.rows, k // self.rows
        owner = (self.count - 1 - k) % self.cols
        if p < 2:
            return owner
        return (owner + (-self.stride if r < self.rows // 2 else self.stride)) % self.cols

    def solver_second(self, k):
        r, p = k % self.rows, k // self.rows
        if self.own_mirror(r):
            if k == 0 or k > self.count - k:
                return None
            return (self.count - k) % self.cols
        return (self.solver_first(k) + 1) % self.cols

    def solving(self, d):
        found = {}
        for k in range(self.count):
            c = self.solver_first(k) if d < self.count else self.solver_second(k)
            if c is not None:
                assert (k % self.rows, c) not in found
                found[(k % self.rows, c)] = k
        return found


def solution(mesh):
    rows, cols = mesh.shape["row"], mesh.shape["col"]
    plan = Plan(rows, cols, 4, 2)
    count, line, stride = plan.count, plan.line, plan.stride
    first, second = plan.solving(count - 1), plan.solving(count)

    def lookup(function):
        return jnp.asarray(plan.table(function))[lax.axis_index("row"), lax.axis_index("col")]

    def send(value, moves):
        pairs = [(s[0] * cols + s[1], t[0] * cols + t[1]) for s, t in moves]
        assert len({s for s, _ in pairs}) == len(pairs) == len({t for _, t in pairs})
        return lax.ppermute(value, AXES, pairs)

    def spread(block, sources, residue):
        got = [block]
        for t in range(1, line):
            got.append(send(block, [((r, c), (r, (c + t * stride) % cols)) for r, c in sources]))
        on_line = lookup(lambda r, c: c % stride == residue[r])
        result = []
        for t in range(line):
            total = got[t]
            out = total
            for step in range(1, stride):
                moves = []
                for r, c in sources:
                    at = (c + t * stride) % cols
                    moves.append(((r, at), (r, at // stride * stride + (at + step) % stride)))
                arrived = send(total, moves)
                mine = lookup(lambda r, c, step=step: c % stride == (residue[r] + step) % stride)
                out = jnp.where(mine, arrived, out)
            result.append(out)
        return jnp.stack(result)

    def local(reversed_rows, state, basis, eigval):
        width = state.shape[2]
        running = state.reshape(4, width, 2, width)
        panel = reversed_rows.reshape(4, width, 2, width)
        own_basis = basis.reshape(4, width, width)
        own_values = eigval.reshape(4, width)

        def block(array, index):
            found = lax.dynamic_slice(array, (index // 2, 0, index % 2, 0), (1, width, 1, width))
            return found.reshape(width, width)

        def slot(k, d):
            _, p, q = plan.place(k, d)
            return 2 * p + q

        def eigen(index):
            vectors = lax.dynamic_index_in_dim(own_basis, index, 0, keepdims=False)
            values = lax.dynamic_index_in_dim(own_values, index, 0, keepdims=True)
            return vectors, values

        def packed(index):
            vectors, values = eigen(index)
            return jnp.concatenate([vectors, jnp.broadcast_to(values, (8, width))], axis=0)

        def unpacked(message):
            return message[:width], message[width : width + 1]

        def gather(d, solving, pick):
            hand, mirrored = [], ([], [])
            hand_slot, mirror_slot = {}, ({}, {})
            for device, k in solving.items():
                owner, p, q = plan.place(k, d)
                if owner != device:
                    hand.append((owner, device))
                    hand_slot[owner] = 2 * p + q
                owner, p, q = plan.place(d - k, d)
                if owner != device:
                    mirrored[p // 2].append((owner, device))
                    mirror_slot[p // 2][owner] = 2 * p + q
            handed = send(pick(lookup(lambda r, c: hand_slot.get((r, c), 0))), hand)
            own = pick(
                lookup(lambda r, c: slot(first_or(solving, (r, c), d), d) if is_own(solving, (r, c), d) else 0)
            )
            own = jnp.where(lookup(lambda r, c: is_own(solving, (r, c), d)), own, handed)
            parts = []
            for side in range(2):
                parts.append(
                    send(pick(lookup(lambda r, c: mirror_slot[side].get((r, c), 0))), mirrored[side])
                )
            mirror = parts[0] + parts[1]

            def at_home(r, c):
                k = solving.get((r, c))
                return k is not None and plan.place(d - k, d)[0] == (r, c)

            if any(at_home(r, c) for r in range(rows) for c in range(cols)):
                near = pick(lookup(lambda r, c: slot(d - solving[(r, c)], d) if at_home(r, c) else 0))
                mirror = jnp.where(lookup(at_home), near, mirror)
            return own, mirror

        def first_or(solving, device, d):
            return solving[device]

        def is_own(solving, device, d):
            k = solving.get(device)
            return k is not None and plan.place(k, d)[0] == device

        def solve(right_side, near, far):
            inner = product(near[0].T, right_side)
            inner = product(inner, far[0])
            inner = inner / (near[1].reshape(width, 1) + far[1].reshape(1, width))
            return product(product(near[0], inner), far[0].T)

        far = send(
            packed(
                lookup(
                    lambda r, c: (count - 1 - first[(rows - 1 - r, c)]) // rows
                    if (rows - 1 - r, c) in first
                    else 0
                )
            ),
            [((rows - 1 - r, c), (r, c)) for r, c in first],
        )
        own, mirror = gather(count - 1, first, lambda index: block(running, index))

        def both(index):
            return jnp.stack([block(running, index), block(panel, index)])

        own_second, mirror_second = gather(count, second, both)
        crossing = [device for device in second if not plan.own_mirror(device[0])]

        def far_slot(r, c):
            k = second.get(((-r) % rows, c))
            return 0 if k is None else (count - k) // rows

        far_second = send(packed(lookup(far_slot)), [(((-r) % rows, c), (r, c)) for r, c in crossing])
        within = lookup(lambda r, c: plan.own_mirror(r))
        near_far = packed(lookup(far_slot))
        far_second = jnp.where(within, near_far, far_second)

        moved = send(panel, [((r, c), ((r + 1) % rows, c)) for r in range(rows) for c in range(cols)])
        rolled = jnp.concatenate([jnp.zeros_like(moved[:1]), moved[:-1]], axis=0)
        next_panel = jnp.where(lax.axis_index("row") == 0, rolled, moved)

        near = eigen(lookup(lambda r, c: first.get((r, c), 0) // rows))
        solved_first = solve(own + mirror.T, near, unpacked(far))

        def first_device(k):
            return (k % rows, plan.solver_first(k))

        direct = [(first_device(k), device) for device, k in second.items()]
        left = send(solved_first, direct)
        cross = [
            (first_device(count - k), device)
            for device, k in second.items()
            if plan.own_mirror(device[0]) and 2 * k != count
        ]
        right = send(solved_first, cross)
        halfway = lookup(lambda r, c: second.get((r, c), 0) * 2 == count)
        right = jnp.where(halfway, left, right).T
        beside = send(
            solved_first,
            [(first_device(k - 1), device) for device, k in second.items() if not plan.own_mirror(device[0])],
        )
        right = jnp.where(within, right, beside)
        change = product(left, own_second[1])
        change_mirror = product(mirror_second[1].T, right)
        right_side = own_second[0] - change + mirror_second[0].T - change_mirror
        near = eigen(lookup(lambda r, c: second.get((r, c), 0) // rows))
        solved_second = solve(right_side, near, unpacked(far_second))

        residue = [plan.solver_first(r) % stride for r in range(rows)]
        line_first = spread(solved_first, list(first), residue)
        residue_second = [next(c for q, c in second if q == r) % stride for r in range(rows)]
        line_second = spread(solved_second, list(second), residue_second)

        def shift_from(c, source):
            return (c // stride - source // stride) % line

        col = lax.axis_index("col")
        first_blocks, second_blocks = [], []
        for p in range(4):
            index = lookup(lambda r, c: shift_from(c, plan.solver_first(p * rows + r)))
            first_blocks.append(lax.dynamic_index_in_dim(line_first, index, 0, keepdims=False))

            def second_index(r, c):
                k = p * rows + r
                at = plan.solver_second(k)
                if at is None:
                    at = plan.solver_second(count - k) if k > 0 else c
                return shift_from(c, at)

            found = lax.dynamic_index_in_dim(
                line_second, lookup(second_index), 0, keepdims=False
            )
            turned = lookup(lambda r, c: plan.solver_second(p * rows + r) is None)
            second_blocks.append(jnp.where(turned, found.T, found))

        ids = jnp.arange(4, dtype=jnp.int32) * rows + lax.axis_index("row")
        columns = jnp.arange(2, dtype=jnp.int32) * cols + col
        for step, (blocks, rows_of_a) in enumerate(
            ((first_blocks, panel), (second_blocks, next_panel))
        ):
            partners = count - 1 + step - ids
            reaches = (columns[None, :] > partners[:, None]) & (partners < count)[:, None]
            changes = jnp.einsum(
                "rab,rbcd->racd",
                jnp.stack(blocks),
                rows_of_a,
                precision=PRECISION,
                preferred_element_type=jnp.float32,
            )
            running = running - jnp.where(reaches[:, None, :, None], changes, 0.0)
        for step, blocks in enumerate((first_blocks, second_blocks)):
            partners = count - 1 + step - ids
            placed = (columns[None, :] == partners[:, None])[:, None, :, None]
            running = jnp.where(placed, jnp.stack(blocks)[:, :, None, :], running)
        return running.reshape(state.shape)

    placed = (
        P(None, "row", None, None, "col", None),
        P(None, "row", None, None, "col", None),
        P(None, "row", None, None),
        P(None, "row", None),
    )
    return jax.shard_map(
        local,
        mesh=mesh,
        in_specs=placed,
        out_specs=P(None, "row", None, None, "col", None),
        check_vma=False,
    )
```

```python
import numpy as np
import jax
import jax.numpy as jnp
from jax import lax
from jax.experimental import pallas as pl
from jax.experimental.pallas import tpu as pltpu
from jax.sharding import PartitionSpec as P

AXES = ("row", "col")
LANES = 128
LIMIT = 40 * 1024 * 1024


def product(first, second, dims=((1,), (0,))):
    return lax.dot_general(
        first,
        second,
        (dims, ((), ())),
        precision=lax.Precision.HIGHEST,
        preferred_element_type=jnp.float32,
    )


class Plan:
    def __init__(self, rows, cols, block_rows, block_cols):
        self.rows, self.cols = rows, cols
        self.count = block_rows * rows
        assert block_rows == 4 and block_cols == 2 and self.count == block_cols * cols
        self.line = 4
        self.stride = cols // self.line
        self.devices = [(r, c) for r in range(rows) for c in range(cols)]
        self.first = self.solving(self.solver_first)
        self.second = self.solving(self.solver_second)

    def own_mirror(self, r):
        return r == (-r) % self.rows

    def place(self, k, d):
        m = d - k
        return (k % self.rows, m % self.cols), 2 * (k // self.rows) + m // self.cols

    def turn(self, r):
        return -1 if self.own_mirror(r) else 1

    def step(self, r, c, by):
        return c // self.stride * self.stride + (c + by * self.turn(r)) % self.stride

    def shift(self, c, by):
        return (c + by * self.stride) % self.cols

    def solver_first(self, k):
        r, p = k % self.rows, k // self.rows
        owner = (self.count - 1 - k) % self.cols
        if p < 2:
            return owner
        return self.shift(owner, -1 if r < self.rows // 2 else 1)

    def solver_second(self, k):
        r = k % self.rows
        if self.own_mirror(r) and (k == 0 or 2 * k > self.count):
            return None
        return self.step(r, self.solver_first(k), 1)

    def solving(self, solver):
        found = {}
        for k in range(self.count):
            c = solver(k)
            if c is not None:
                assert (k % self.rows, c) not in found
                found[(k % self.rows, c)] = k
        return found

    def wants(self, k, d, c):
        return d - k < self.count and self.cols + c >= d - k

    def uses(self, k, d, device):
        r, c = device
        if k % self.rows == r and self.wants(k, d, c):
            return True
        return d == self.count and (d - k) % self.rows == r and k % self.rows == r and self.wants(d - k, d, c)


class Table:
    def __init__(self, plan):
        self.plan, self.columns, self.names = plan, [], {}

    def add(self, name, function):
        self.names[name] = len(self.columns)
        self.columns.append([int(function(device)) for device in plan_devices(self.plan)])

    def array(self):
        return np.asarray(self.columns, np.int32).T.reshape(-1)

    def reader(self, ref):
        device = lax.axis_index("row") * self.plan.cols + lax.axis_index("col")
        return lambda name: ref[device * len(self.columns) + self.names[name]]


def plan_devices(plan):
    return plan.devices


def solution(mesh):
    rows, cols = mesh.shape["row"], mesh.shape["col"]
    plan = Plan(rows, cols, 4, 2)
    count, line, stride = plan.count, plan.line, plan.stride
    first, second = plan.first, plan.second
    table = Table(plan)

    def checked(moves):
        assert len({s for s, _ in moves}) == len(moves) == len({t for _, t in moves})
        return moves

    def send(value, moves):
        pairs = [(s[0] * cols + s[1], t[0] * cols + t[1]) for s, t in checked(moves)]
        return lax.ppermute(value, AXES, pairs)

    def operand_moves(name, d, solving):
        hand, mirror = [], ([], [])
        slots = {"hand": {}, "mirror0": {}, "mirror1": {}}
        for device, k in solving.items():
            owner, slot = plan.place(k, d)
            if owner != device:
                hand.append((owner, device))
                slots["hand"][owner] = slot
            owner, slot = plan.place(d - k, d)
            assert owner != device
            mirror[slot // 4].append((owner, device))
            slots["mirror%d" % (slot // 4)][owner] = slot
        for part, found in slots.items():
            table.add(name + part, lambda device: found.get(device, 0))
        local = lambda device: device in solving and plan.place(solving[device], d)[0] == device
        table.add(name + "local", local)
        table.add(name + "own", lambda device: plan.place(solving[device], d)[1] if local(device) else 0)
        table.add(name + "near", lambda device: solving.get(device, 0) // rows)
        table.add(name + "solves", lambda device: device in solving)
        return checked(hand), checked(mirror[0]), checked(mirror[1])

    hand_first, mirror_first0, mirror_first1 = operand_moves("first_", count - 1, first)
    hand_second, mirror_second0, mirror_second1 = operand_moves("second_", count, second)

    far_first = [((rows - 1 - r, c), (r, c)) for r, c in first]
    table.add(
        "first_far",
        lambda device: (count - 1 - first.get((rows - 1 - device[0], device[1]), 0)) // rows,
    )
    far_second = [((-r % rows, c), (r, c)) for r, c in second if not plan.own_mirror(r)]

    def far_slot(device):
        k = second.get((-device[0] % rows, device[1]), 1)
        return (count - k) // rows

    table.add("second_far", far_slot)
    table.add("within", lambda device: plan.own_mirror(device[0]))
    table.add("halfway", lambda device: 2 * second.get(device, 0) == count)

    def at_first(k):
        return (k % rows, plan.solver_first(k))

    cross = [
        (at_first(count - k), device)
        for device, k in second.items()
        if plan.own_mirror(device[0]) and 2 * k != count
    ]
    beside = [(at_first(k - 1), device) for device, k in second.items() if not plan.own_mirror(device[0])]

    def spread_moves(d, solving):
        shifts = []
        steps = {}
        for by in range(1, line):
            moves = []
            for (r, c), k in solving.items():
                at = plan.shift(c, by)
                group = [(r, plan.step(r, at, step)) for step in range(stride)]
                if any(plan.uses(k, d, device) for device in group):
                    moves.append(((r, c), (r, at)))
            shifts.append(moves)
        for by in range(line):
            for step in range(1, stride):
                moves = []
                for (r, c), k in solving.items():
                    at = plan.shift(c, by)
                    target = (r, plan.step(r, at, step))
                    direct = d < count and by == 0 and second.get(target) in (k, count - k)
                    if plan.uses(k, d, target) or direct or (d < count and by == 0 and step == 1):
                        moves.append(((r, at), target))
                steps[by, step] = moves
        return shifts, steps

    shifts_first, steps_first = spread_moves(count - 1, first)
    shifts_second, steps_second = spread_moves(count, second)

    for p in range(4):

        def index_first(device, p=p):
            return (device[1] // stride - plan.solver_first(p * rows + device[0]) // stride) % line

        table.add("first_index%d" % p, index_first)

        def turned(device, p=p):
            k = p * rows + device[0]
            return k > 0 and plan.solver_second(k) is None

        def index_second(device, p=p):
            k = p * rows + device[0]
            if k == 0:
                return 0
            at = plan.solver_second(count - k if turned(device, p) else k)
            return (device[1] // stride - at // stride) % line

        table.add("second_turned%d" % p, turned)
        table.add("second_index%d" % p, index_second)

    def reached(device, p, q):
        k = p * rows + device[0]
        return 0 < k and q * cols + device[1] > count - k

    common = [(p, q) for p in range(4) for q in range(2) if reached((rows // 2, cols // 2), p, q)]
    seldom = [
        (p, q)
        for p in range(4)
        for q in range(2)
        if (p, q) not in common and any(reached(device, p, q) for device in plan.devices)
    ]

    def panel_moves(slots):
        return [
            ((((r - 1) % rows), c), (r, c))
            for r, c in plan.devices
            if any(reached((r, c), p, q) for p, q in slots)
        ]

    def source_row(p):
        name = "panel%d" % p
        if name not in table.names:
            table.add(name, lambda device: p - 1 if device[0] == rows - 1 and p > 0 else p)
        return name

    for p in range(4):
        source_row(p)
    constants = table.array()

    def local(reversed_rows, state, basis, eigval):
        width = state.shape[2]
        halves = width // LANES
        stripe = 2 * halves
        running = state.reshape(4 * width * stripe, LANES)
        panel = reversed_rows.reshape(4 * width * stripe, LANES)
        own_basis = basis.reshape(4, width, width)
        own_values = eigval.reshape(4, width)
        numbers = jnp.asarray(constants)
        block_shape = jax.ShapeDtypeStruct((width, width), jnp.float32)
        pair_shape = jax.ShapeDtypeStruct((2 * width, width), jnp.float32)
        eigen_shape = jax.ShapeDtypeStruct((width + 8, width), jnp.float32)

        def where_at(slot, half):
            start = slot // 2 * (width * stripe) + slot % 2 * halves + half
            return pl.ds(start, width, stride=stripe)

        def read(ref, slot):
            parts = [ref[where_at(slot, half), :] for half in range(halves)]
            return jnp.concatenate(parts, axis=1) if halves > 1 else parts[0]

        def write(ref, slot, value):
            for half in range(halves):
                ref[where_at(slot, half), :] = value[:, half * LANES : (half + 1) * LANES]

        def call(body, outputs, *operands, flops=0):
            whole = pl.BlockSpec(memory_space=pltpu.VMEM)
            moved = sum(4 * int(np.prod(o.shape)) for o in (*operands, *outputs))
            return pl.pallas_call(
                body,
                out_shape=outputs,
                in_specs=[pl.BlockSpec(memory_space=pltpu.SMEM)] + [whole] * len(operands),
                out_specs=[whole] * len(outputs),
                compiler_params=pltpu.CompilerParams(vmem_limit_bytes=LIMIT),
                cost_estimate=pl.CostEstimate(flops=flops, bytes_accessed=moved, transcendentals=0),
            )(numbers, *operands)

        def put_eigen(target, basis_ref, values_ref, index):
            target[:width, :] = basis_ref[index]
            target[width:, :] = jnp.broadcast_to(values_ref[pl.ds(index, 1), :], (8, width))

        def pack_first(numbers_ref, state_ref, basis_ref, values_ref, mirror0, mirror1, hand, far, own):
            at = table.reader(numbers_ref)
            mirror0[...] = read(state_ref, at("first_mirror0"))
            mirror1[...] = read(state_ref, at("first_mirror1"))
            hand[...] = read(state_ref, at("first_hand"))
            put_eigen(far, basis_ref, values_ref, at("first_far"))
            value = read(state_ref, at("first_own"))
            own[...] = jnp.where(at("first_local") == 1, value, 0.0)

        def pack_second(
            numbers_ref, state_ref, panel_ref, basis_ref, values_ref,
            mirror0, mirror1, hand, far, own, often, rarely,
        ):
            at = table.reader(numbers_ref)
            for target, name in ((mirror0, "mirror0"), (mirror1, "mirror1"), (hand, "hand"), (own, "own")):
                slot = at("second_" + name)
                pair = (read(state_ref, slot), read(panel_ref, slot))
                for index, value in enumerate(pair):
                    if name == "own":
                        value = jnp.where(at("second_local") == 1, value, 0.0)
                    target[index * width : (index + 1) * width, :] = value
            put_eigen(far, basis_ref, values_ref, at("second_far"))
            for target, slots in ((often, common), (rarely, seldom)):
                for index, (p, q) in enumerate(slots):
                    slot = 2 * at("panel%d" % p) + q
                    target[index * width : (index + 1) * width, :] = read(panel_ref, slot)

        def column(values):
            return jnp.broadcast_to(values, (width, width)).T

        def solve(right_side, near, near_values, far, far_values):
            inner = product(near.T, right_side)
            inner = product(inner, far)
            inner = inner / (column(near_values) + far_values)
            return product(product(near, inner), far, ((1,), (1,)))

        def solve_first(
            numbers_ref, own, hand, mirror0, mirror1, far, basis_ref, values_ref, out
        ):
            at = table.reader(numbers_ref)
            right_side = own[...] + hand[...] + (mirror0[...] + mirror1[...]).T
            index = at("first_near")
            found = solve(
                right_side,
                basis_ref[index],
                values_ref[pl.ds(index, 1), :],
                far[:width, :],
                far[width : width + 1, :],
            )
            out[...] = jnp.where(at("first_solves") == 1, found, 0.0)

        def solve_second(
            numbers_ref, own, hand, mirror0, mirror1, far, left, cross_ref, beside_ref,
            basis_ref, values_ref, out,
        ):
            at = table.reader(numbers_ref)
            upper, lower = slice(0, width), slice(width, 2 * width)
            halfway = jnp.where(at("halfway") == 1, left[...], 0.0)
            right = (cross_ref[...] + halfway).T + beside_ref[...]
            own_side = own[upper, :] + hand[upper, :]
            own_side = own_side - product(left[...], own[lower, :] + hand[lower, :])
            across = (mirror0[lower, :] + mirror1[lower, :]).T
            mirror_side = (mirror0[upper, :] + mirror1[upper, :]).T - product(across, right)
            index = at("second_near")
            within = at("within") == 1
            far_index = at("second_far")
            far_basis = jnp.where(within, basis_ref[far_index], far[:width, :])
            far_values = jnp.where(within, values_ref[pl.ds(far_index, 1), :], far[width : width + 1, :])
            found = solve(
                own_side + mirror_side,
                basis_ref[index],
                values_ref[pl.ds(index, 1), :],
                far_basis,
                far_values,
            )
            out[...] = jnp.where(at("second_solves") == 1, found, 0.0)

        def update(d, name, slots_of):
            def body(numbers_ref, running_ref, *refs):
                at = table.reader(numbers_ref)
                arrived, sources, out, blocks = refs[: line * stride], refs[line * stride : -2], refs[-2], refs[-1]
                for by in range(line):
                    total = arrived[by * stride][...]
                    for step in range(1, stride):
                        total = total + arrived[by * stride + step][...]
                    blocks[by] = total
                row, col = lax.axis_index("row"), lax.axis_index("col")
                for p in range(4):
                    partner = d - (p * rows + row)
                    index = at("%s_index%d" % (name, p))
                    for q in range(2):
                        here = q * cols + col
                        slot = 2 * p + q
                        rest = read(running_ref, slot)
                        write(out, slot, rest)
                        rows_of_a = slots_of(sources, p, q)

                        if rows_of_a is not None:

                            @pl.when((here > partner) & (partner < count))
                            def _():
                                taken = blocks[index]
                                if name == "second":
                                    taken = jnp.where(at("second_turned%d" % p) == 1, taken.T, taken)
                                write(out, slot, rest - product(taken, rows_of_a()))

                        @pl.when(here == partner)
                        def _():
                            taken = blocks[index]
                            if name == "second":
                                taken = jnp.where(at("second_turned%d" % p) == 1, taken.T, taken)
                            write(out, slot, taken)

            def run(running, arrived, sources):
                whole = pl.BlockSpec(memory_space=pltpu.VMEM)
                operands = (running, *arrived, *sources)
                return pl.pallas_call(
                    body,
                    out_shape=jax.ShapeDtypeStruct(running.shape, jnp.float32),
                    in_specs=[pl.BlockSpec(memory_space=pltpu.SMEM)] + [whole] * len(operands),
                    out_specs=whole,
                    scratch_shapes=[pltpu.VMEM((line, width, width), jnp.float32)],
                    compiler_params=pltpu.CompilerParams(vmem_limit_bytes=LIMIT),
                    cost_estimate=pl.CostEstimate(
                        flops=16 * width**3 * 6, bytes_accessed=8 * running.size, transcendentals=0
                    ),
                )(numbers, *operands)

            return run

        def own_panel(sources, p, q):
            return lambda: read(sources[0], 2 * p + q)

        def next_panel(sources, p, q):
            for ref, slots in zip(sources, (common, seldom)):
                if (p, q) in slots:
                    index = slots.index((p, q))
                    return lambda: ref[index * width : (index + 1) * width, :]
            return None

        def forward(blocks, steps):
            arrived = []
            for by in range(line):
                arrived.append(blocks[by])
                for step in range(1, stride):
                    arrived.append(send(blocks[by], steps[by, step]))
            return arrived

        solve_flops = 4 * 2 * 6 * width**3

        mirror0, mirror1, hand, far, own = call(
            pack_first,
            [block_shape] * 3 + [eigen_shape, block_shape],
            running, own_basis, own_values,
        )
        mirror0 = send(mirror0, mirror_first0)
        mirror1 = send(mirror1, mirror_first1)
        hand = send(hand, hand_first)
        far = send(far, far_first)

        later = call(
            pack_second,
            [pair_shape] * 3
            + [eigen_shape, pair_shape]
            + [
                jax.ShapeDtypeStruct((len(slots) * width, width), jnp.float32)
                for slots in (common, seldom)
            ],
            running, panel, own_basis, own_values,
        )
        later_mirror0 = send(later[0], mirror_second0)
        later_mirror1 = send(later[1], mirror_second1)
        later_hand = send(later[2], hand_second)
        later_far = send(later[3], far_second)
        later_own = later[4]
        often = send(later[5], panel_moves(common))
        rarely = send(later[6], panel_moves(seldom))

        (solved,) = call(
            solve_first, [block_shape], own, hand, mirror0, mirror1, far, own_basis, own_values,
            flops=solve_flops,
        )
        left = send(solved, steps_first[0, 1])
        next_to = send(solved, beside)
        crossed = send(solved, cross)
        blocks = [solved] + [send(solved, moves) for moves in shifts_first]

        (solved_next,) = call(
            solve_second, [block_shape],
            later_own, later_hand, later_mirror0, later_mirror1, later_far,
            left, crossed, next_to, own_basis, own_values,
            flops=solve_flops + solve_flops // 2,
        )
        arrived = [blocks[0], left] + [send(blocks[0], steps_first[0, s]) for s in range(2, stride)]
        arrived += forward(blocks, steps_first)[stride:]
        running = update(count - 1, "first", own_panel)(running, arrived, [panel])

        blocks = [solved_next] + [send(solved_next, moves) for moves in shifts_second]
        arrived = forward(blocks, steps_second)
        running = update(count, "second", next_panel)(running, arrived, [often, rarely])
        return running.reshape(state.shape)

    placed = (
        P(None, "row", None, None, "col", None),
        P(None, "row", None, None, "col", None),
        P(None, "row", None, None),
        P(None, "row", None),
    )
    return jax.shard_map(
        local,
        mesh=mesh,
        in_specs=placed,
        out_specs=P(None, "row", None, None, "col", None),
        check_vma=False,
    )
```

```python
import numpy as np
import jax
import jax.numpy as jnp
from jax import lax
from jax.experimental import pallas as pl
from jax.experimental.pallas import tpu as pltpu
from jax.sharding import PartitionSpec as P

AXES = ("row", "col")
LANES = 128
LIMIT = 40 * 1024 * 1024
GATE_SECOND = "none"
GATE_SPREAD = "next"
GATE_PANEL = "next"


def product(first, second, dims=((1,), (0,))):
    return lax.dot_general(
        first,
        second,
        (dims, ((), ())),
        precision=lax.Precision.HIGHEST,
        preferred_element_type=jnp.float32,
    )


class Plan:
    line = 4

    def __init__(self, rows, cols, block_rows, block_cols):
        self.rows, self.cols = rows, cols
        self.count = block_rows * rows
        assert block_rows == 4 and block_cols == 2 and self.count == block_cols * cols
        self.stride = cols // self.line

    def within(self, r):
        return r % (self.rows // 2) == 0

    def sign(self, r):
        return 1 - 2 * ((2 * r) // self.rows)

    def solver(self, r, p):
        order = 2 * (p % 2) + p // 2
        return (self.cols - 1 - r - self.sign(r) * order * self.stride) % self.cols

    def solves(self, r, c):
        return c % self.stride == (self.cols - 1 - r) % self.stride

    def local_row(self, r, c):
        order = (self.sign(r) * (self.cols - 1 - r - c)) % self.cols // self.stride
        return 2 * (order % 2) + order // 2

    def local_at(self, d, c, q):
        return (d - q * self.cols - c) // self.rows

    def shift(self, c, by):
        return (c + by * self.stride) % self.cols

    def step(self, c, by):
        return c // self.stride * self.stride + (c + by) % self.stride


def solution(mesh):
    rows, cols = mesh.shape["row"], mesh.shape["col"]
    plan = Plan(rows, cols, 4, 2)
    count, line, stride = plan.count, plan.line, plan.stride
    devices = [(r, c) for r in range(rows) for c in range(cols)]
    first = {(r, c): plan.local_row(r, c) * rows + r for r, c in devices if plan.solves(r, c)}
    assert sorted(first.values()) == list(range(count))
    assert all(plan.solver(r, k // rows) == c for (r, c), k in first.items())
    second = {
        device: k
        for device, k in first.items()
        if not (plan.within(device[0]) and (k == 0 or 2 * k > count))
    }

    def send(value, moves):
        assert len({s for s, _ in moves}) == len(moves) == len({t for _, t in moves})
        return lax.ppermute(value, AXES, [(s[0] * cols + s[1], t[0] * cols + t[1]) for s, t in moves])

    def after(value, *others):
        return lax.optimization_barrier((value, *others))[0] if others else value

    def operand_moves(d, solving):
        hand, mirror = ([], []), ([], [])
        for device, k in solving.items():
            for moves, i in ((hand, k), (mirror, d - k)):
                owner = (i % rows, (d - i) % cols)
                assert plan.local_at(d, owner[1], (d - i) // cols) == i // rows
                if owner != device:
                    moves[(d - i) // cols].append((owner, device))
                else:
                    assert moves is hand and d < count and i // rows < 2
        return hand, mirror

    hand_first, mirror_first = operand_moves(count - 1, first)
    assert not hand_first[1]
    hand_second, mirror_second = operand_moves(count, second)
    far_first = [((rows - 1 - r, c), (r, c)) for r, c in first]
    far_second = [((-r % rows, c), (r, c)) for r, c in second if not plan.within(r)]

    def solver_of(k):
        return (k % rows, plan.solver(k % rows, k // rows))

    beside = [(solver_of(k - 1), device) for device, k in second.items() if not plan.within(device[0])]
    for (r, c), k in second.items():
        if plan.within(r) and 2 * k != count:
            assert solver_of(count - k) == (r, plan.shift(c, -1))

    def wants(k, d, c):
        return d - k < count and cols + c >= d - k

    def uses(k, d, device):
        r, c = device
        return wants(k, d, c) or (d == count and plan.within(r) and wants(d - k, d, c))

    def spread_moves(d, solving):
        shifts, steps = [], {}
        for by in range(1, line):
            moves = []
            for (r, c), k in solving.items():
                at = plan.shift(c, by)
                group = [(r, plan.step(at, step)) for step in range(stride)]
                direct = d < count and by == 1 and second.get((r, at)) == count - k
                if direct or any(uses(k, d, device) for device in group):
                    moves.append(((r, c), (r, at)))
            shifts.append(moves)
        for by in range(line):
            for step in range(1, stride):
                moves = []
                for (r, c), k in solving.items():
                    at = plan.shift(c, by)
                    target = (r, plan.step(at, step))
                    if uses(k, d, target):
                        moves.append(((r, at), target))
                steps[by, step] = moves
        return shifts, steps

    shifts_first, steps_first = spread_moves(count - 1, first)
    shifts_second, steps_second = spread_moves(count, second)

    def reached(device, p, q):
        k = p * rows + device[0]
        return 0 < k and q * cols + device[1] > count - k

    slots = [(p, q) for p in range(4) for q in range(2)]
    common = [s for s in slots if reached((rows // 2, cols // 2), *s)]
    seldom = [s for s in slots if s not in common and any(reached(device, *s) for device in devices)]

    def panel_moves(chosen):
        return [
            (((r - 1) % rows, c), (r, c)) for r, c in devices if any(reached((r, c), *s) for s in chosen)
        ]

    def local(reversed_rows, state, basis, eigval):
        width = state.shape[2]
        halves = width // LANES
        stripe = 2 * halves
        slab = width * stripe
        running = state.reshape(4 * slab, LANES)
        panel = reversed_rows.reshape(4 * slab, LANES)
        own_basis = basis.reshape(4, width, width)
        own_values = eigval.reshape(4 * halves, LANES)
        block_shape = jax.ShapeDtypeStruct((width, width), jnp.float32)
        pair_shape = jax.ShapeDtypeStruct((2 * width, width), jnp.float32)
        eigen_shape = jax.ShapeDtypeStruct((width + 8, width), jnp.float32)
        vmem = pl.BlockSpec(memory_space=pltpu.VMEM)
        hbm = pl.BlockSpec(memory_space=pltpu.HBM)

        def where_at(p, q, half):
            return pl.ds(p * slab + q * halves + half, width, stride=stripe)

        def joined(parts):
            return jnp.concatenate(parts, axis=1) if halves > 1 else parts[0]

        def read(ref, p, q):
            return joined([ref[where_at(p, q, half), :] for half in range(halves)])

        def write(ref, p, q, value):
            for half in range(halves):
                ref[where_at(p, q, half), :] = value[:, half * LANES : (half + 1) * LANES]

        def values_at(ref, p):
            return joined([ref[pl.ds(p * halves + half, 1), :] for half in range(halves)])

        def here():
            return lax.axis_index("row"), lax.axis_index("col")

        def call(body, outputs, operands, specs=None, scratch=(), flops=0):
            moved = sum(4 * int(np.prod(o.shape)) for o in (*operands, *outputs))
            return pl.pallas_call(
                body,
                out_shape=outputs,
                in_specs=specs or [vmem] * len(operands),
                out_specs=[vmem] * len(outputs),
                scratch_shapes=scratch,
                compiler_params=pltpu.CompilerParams(vmem_limit_bytes=LIMIT),
                cost_estimate=pl.CostEstimate(flops=flops, bytes_accessed=moved, transcendentals=0),
            )(*operands)

        def local_at(d, c, q):
            return jnp.clip(plan.local_at(d, c, q), 0, 3)

        def pack_first(state_ref, basis_ref, values_ref, upper, lower, far, slabs, values, sems):
            r, c = here()
            index = 3 - plan.local_row(rows - 1 - r, c)
            places = [local_at(count - 1, c, q) for q in range(2)]
            copies = [
                pltpu.make_async_copy(
                    state_ref.at[pl.ds(pl.multiple_of(places[q] * slab, slab), slab)], slabs.at[q], sems.at[q]
                )
                for q in (1, 0)
            ]
            copies.append(pltpu.make_async_copy(basis_ref.at[index], far.at[pl.ds(0, width)], sems.at[2]))
            copies.append(pltpu.make_async_copy(values_ref, values, sems.at[3]))
            for copy in copies:
                copy.start()
            copies[0].wait()
            upper[...] = read(slabs.at[1], 0, 1)
            copies[1].wait()
            lower[...] = read(slabs.at[0], 0, 0)
            copies[3].wait()
            far[width:, :] = jnp.broadcast_to(values_at(values, index), (8, width))
            copies[2].wait()

        def pack_second(state_ref, panel_ref, basis_ref, values_ref, upper, lower, far, often, rarely):
            r, c = here()
            for target, q in ((upper, 1), (lower, 0)):
                p = local_at(count, c, q)
                target[:width, :] = read(state_ref, p, q)
                target[width:, :] = read(panel_ref, p, q)
            opposite = lax.rem(rows - r, rows)
            k = plan.local_row(opposite, c) * rows + opposite
            index = jnp.clip((count - k) // rows, 0, 3)
            far[:width, :] = basis_ref[index]
            far[width:, :] = jnp.broadcast_to(values_at(values_ref, index), (8, width))
            last = (r == rows - 1).astype(jnp.int32)
            for target, chosen in ((often, common), (rarely, seldom)):
                for index, (p, q) in enumerate(chosen):
                    source = jnp.maximum(p - last, 0)
                    target[index * width : (index + 1) * width, :] = read(panel_ref, source, q)

        def column(values):
            return jnp.broadcast_to(values, (width, width)).T

        def solve(right_side, near, near_values, far, far_values):
            inner = product(near.T, right_side)
            inner = product(inner, far)
            inner = inner / (column(near_values) + far_values)
            return product(product(near, inner), far, ((1,), (1,)))

        def solve_first(upper, hand, mirror0, mirror1, far, basis_ref, values_ref, out):
            r, c = here()
            p = plan.local_row(r, c)
            solves = plan.solves(r, c)
            own = jnp.where(solves & (p < 2), upper[...], 0.0) + hand[...]
            right_side = own + (mirror0[...] + mirror1[...]).T
            found = solve(
                right_side,
                basis_ref[p],
                values_at(values_ref, p),
                far[:width, :],
                far[width : width + 1, :],
            )
            out[...] = jnp.where(solves, found, 0.0)

        def solve_second(
            hand0, hand1, mirror0, mirror1, far, left, shifted, beside_ref, basis_ref, values_ref, out
        ):
            r, c = here()
            p = plan.local_row(r, c)
            k = p * rows + r
            within = plan.within(r)
            halfway = 2 * k == count
            top, bottom = slice(0, width), slice(width, 2 * width)
            turned = jnp.where(halfway, left[...], shifted[...]).T
            right = jnp.where(within, turned, beside_ref[...])
            own_side = hand0[top, :] + hand1[top, :]
            own_side = own_side - product(left[...], hand0[bottom, :] + hand1[bottom, :])
            across = (mirror0[bottom, :] + mirror1[bottom, :]).T
            mirror_side = (mirror0[top, :] + mirror1[top, :]).T - product(across, right)
            far_index = jnp.clip((count - k) // rows, 0, 3)
            far_basis = jnp.where(within, basis_ref[far_index], far[:width, :])
            far_values = jnp.where(within, values_at(values_ref, far_index), far[width : width + 1, :])
            found = solve(
                own_side + mirror_side, basis_ref[p], values_at(values_ref, p), far_basis, far_values
            )
            idle = within & ((k == 0) | (2 * k > count))
            out[...] = jnp.where(plan.solves(r, c) & jnp.logical_not(idle), found, 0.0)

        def update(d, running, arrived, sources, rows_of_a):
            def body(running_ref, *refs):
                r, c = here()
                parts, given = refs[: len(arrived)], refs[len(arrived) : -2]
                out, blocks = refs[-2], refs[-1]
                for by in range(line):
                    total = parts[by * stride][...]
                    for step in range(1, stride):
                        total = total + parts[by * stride + step][...]
                    blocks[by] = total
                for p in range(4):
                    k = p * rows + r
                    partner = d - k
                    turned = plan.within(r) & (2 * k > count)
                    if d < count:
                        turned = jnp.bool_(False)
                    solved_row = jnp.where(turned, jnp.clip(partner // rows, 0, 3), p)
                    index = (c // stride - plan.solver(r, solved_row) // stride) % line

                    def block():
                        found = blocks[index]
                        return found if d < count else jnp.where(turned, found.T, found)

                    for q in range(2):
                        at = q * cols + c
                        old = read(running_ref, p, q)
                        write(out, p, q, old)
                        a_block = rows_of_a(given, p, q)
                        if a_block is not None:

                            @pl.when((at > partner) & (partner < count))
                            def _():
                                write(out, p, q, old - product(block(), a_block()))

                        @pl.when(at == partner)
                        def _():
                            write(out, p, q, block())

            return call(
                body,
                [jax.ShapeDtypeStruct(running.shape, jnp.float32)],
                (running, *arrived, *sources),
                scratch=[pltpu.VMEM((line, width, width), jnp.float32)],
                flops=16 * width**3 * 6,
            )[0]

        def own_rows(given, p, q):
            return lambda: read(given[0], p, q)

        def next_rows(given, p, q):
            for ref, chosen in zip(given, (common, seldom)):
                if (p, q) in chosen:
                    at = chosen.index((p, q)) * width
                    return lambda: ref[at : at + width, :]
            return None

        def forwarded(blocks, steps):
            arrived = []
            for by in range(line):
                arrived.append(blocks[by])
                for step in range(1, stride):
                    arrived.append(send(blocks[by], steps[by, step]))
            return arrived

        solve_flops = 4 * 2 * 6 * width**3

        upper, lower, far = call(
            pack_first,
            [block_shape, block_shape, eigen_shape],
            (running, own_basis, own_values),
            specs=[hbm, hbm, hbm],
            scratch=[
                pltpu.VMEM((2, slab, LANES), jnp.float32),
                pltpu.VMEM((4 * halves, LANES), jnp.float32),
                pltpu.SemaphoreType.DMA((4,)),
            ],
        )
        mirror1 = send(upper, mirror_first[1])
        mirror0 = send(lower, mirror_first[0])
        far = send(far, far_first)
        hand = send(lower, hand_first[0])

        gates = {"none": (), "hand": (hand,), "far": (far,), "all": (hand, far, mirror0, mirror1)}[GATE_SECOND]
        later = call(
            pack_second,
            [pair_shape, pair_shape, eigen_shape]
            + [jax.ShapeDtypeStruct((len(s) * width, width), jnp.float32) for s in (common, seldom)],
            (after(running, *gates), panel, own_basis, own_values),
        )
        hands = [send(later[1], hand_second[0]), send(later[0], hand_second[1])]
        mirrors = [send(later[1], mirror_second[0]), send(later[0], mirror_second[1])]
        far_later = send(later[2], far_second)

        (solved,) = call(
            solve_first,
            [block_shape],
            (upper, hand, mirror0, mirror1, far, own_basis, own_values),
            flops=solve_flops,
        )

        next_to = send(solved, beside)
        shifted = send(solved, shifts_first[0])
        (solved_next,) = call(
            solve_second,
            [block_shape],
            (*hands, *mirrors, far_later, solved, shifted, next_to, own_basis, own_values),
            flops=solve_flops + solve_flops // 2,
        )
        options = {"none": (), "beside": (next_to,), "both": (next_to, shifted), "next": (solved_next,)}
        held = after(solved, *options[GATE_SPREAD])
        blocks = [held, shifted, send(held, shifts_first[1]), send(held, shifts_first[2])]
        often = send(after(later[3], *options[GATE_PANEL]), panel_moves(common))
        rarely = send(after(later[4], *options[GATE_PANEL]), panel_moves(seldom))
        arrived = forwarded(blocks, steps_first)
        running = update(count - 1, running, arrived, [panel], own_rows)

        blocks = [solved_next] + [send(solved_next, moves) for moves in shifts_second]
        arrived = forwarded(blocks, steps_second)
        running = update(count, running, arrived, [often, rarely], next_rows)
        return running.reshape(state.shape)

    placed = (
        P(None, "row", None, None, "col", None),
        P(None, "row", None, None, "col", None),
        P(None, "row", None, None),
        P(None, "row", None),
    )
    return jax.shard_map(
        local,
        mesh=mesh,
        in_specs=placed,
        out_specs=P(None, "row", None, None, "col", None),
        check_vma=False,
    )
```

```python
import numpy as np
import jax
import jax.numpy as jnp
from jax import lax
from jax.experimental import pallas as pl
from jax.experimental.pallas import tpu as pltpu
from jax.sharding import PartitionSpec as P

AXES = ("row", "col")
LANES = 128
LIMIT = 40 * 1024 * 1024
LINE = 4
GATE_SPREAD = "none"
GATE_PANEL = "none"
GATE_FORWARD = "often"
GATE_SOLVE = "none"
PACK_SEEN = None
DIRECT = (True, False)
GATE_LOW = "none"


def product(first, second, dims=((1,), (0,))):
    return lax.dot_general(
        first,
        second,
        (dims, ((), ())),
        precision=lax.Precision.HIGHEST,
        preferred_element_type=jnp.float32,
    )


def solution(mesh):
    rows, cols = mesh.shape["row"], mesh.shape["col"]
    count = 4 * rows
    assert cols == 2 * rows and cols % LINE == 0
    stride = cols // LINE
    devices = [(r, c) for r in range(rows) for c in range(cols)]

    def holds(d, r, c):
        return c % rows == (d - r) % rows

    def local_row(d, c, q):
        return (d - q * cols - c) // rows

    def within(r):
        return r % (rows // 2) == 0

    def shift(c, by):
        return (c + by * stride) % cols

    def step(c, by):
        return c // stride * stride + (c + by) % stride

    first = [device for device in devices if holds(count - 1, *device)]
    second = [device for device in devices if holds(count, *device)]

    def send(value, moves):
        assert len({s for s, _ in moves}) == len(moves) == len({t for _, t in moves})
        return lax.ppermute(value, AXES, [(s[0] * cols + s[1], t[0] * cols + t[1]) for s, t in moves])

    def after(value, *others):
        return lax.optimization_barrier((value, *others))[0] if others else value

    mirror_first = [((rows - 1 - r, cols - 1 - c), (r, c)) for r, c in first]
    mirror_second = [((-r % rows, -c % cols), (r, c)) for r, c in second if r != 0]
    far = [((c % rows, c), (r, c)) for r, c in first]
    far += [((c % rows, step(c, 1)), (r, c)) for r, c in second if not within(r)]
    left = [((r, (c - 1) % cols), (r, c)) for r, c in second]
    above = [(((r - 1) % rows, c), (r, c)) for r, c in second]

    def middle(d, c):
        return (c == 0) & (d == count)

    def solved_row(d, c):
        return local_row(d, c, 0) - 2 * middle(d, c)

    def wants(k, d, c):
        return 0 <= d - k < count and cols + c >= d - k

    def needs(d, source):
        r, c = source
        k = solved_row(d, c) * rows + r
        at_all = range(cols)
        if d == count and within(r):
            return {(r, at) for at in at_all if wants(k, d, at) or wants(d - k, d, at)}
        return {(r, at) for at in at_all if wants(k, d, at)}

    def needs_turned(d, source):
        r, c = source
        if d == count and within(r):
            return set()
        k = d - (solved_row(d, c) * rows + r)
        return {(k % rows, at) for at in range(cols) if wants(k, d, at)}

    def spread_moves(d, sources, direct):
        own, turned = {}, {}
        for source in sources:
            own[source], turned[source] = needs(d, source), needs_turned(d, source)
            if not direct:
                own[source] = own[source] | {(source[0], at) for _, at in turned[source]}
                turned[source] = set()

        def line_moves(by, used, target_row):
            moves = []
            for r, c in sources:
                at = shift(c, by)
                if any((target_row(r), step(at, n)) in used[r, c] for n in range(stride)):
                    moves.append(((r, c), (target_row(r), at)))
            return moves

        def group_moves(half, n, used, target_row):
            moves = []
            for r, c in sources:
                for by in (2 * half, 2 * half + 1):
                    at = shift(c, by)
                    if (target_row(r), step(at, n)) in used[r, c]:
                        moves.append(((target_row(r), at), (target_row(r), step(at, n))))
            return moves

        same, other = (lambda r: r), (lambda r: (d - r) % rows)
        shifts = [line_moves(by, own, same) for by in range(LINE)]
        shifts_turned = [line_moves(by, turned, other) for by in range(LINE)]
        steps, steps_turned = {}, {}
        for half in range(2):
            for n in range(1, stride):
                steps[half, n] = group_moves(half, n, own, same)
                steps_turned[half, n] = group_moves(half, n, turned, other)
        return shifts, shifts_turned, steps, steps_turned

    def across_moves(d, sources):
        targets = set().union(*(needs_turned(d, source) for source in sources))
        return [(((d - t) % rows, c), (t, c)) for t, c in sorted(targets)]

    def reached(device, p, q):
        k = p * rows + device[0]
        return 0 < k and q * cols + device[1] > count - k

    slots = [(p, q) for p in range(4) for q in range(2)]
    common = [s for s in slots if reached((rows // 2, cols // 2), *s)]
    seldom = [s for s in slots if s not in common and any(reached(device, *s) for device in devices)]

    def panel_moves(chosen):
        return [
            (((r - 1) % rows, c), (r, c)) for r, c in devices if any(reached((r, c), *s) for s in chosen)
        ]

    def local(reversed_rows, state, basis, eigval):
        width = state.shape[2]
        halves = width // LANES
        stripe = 2 * halves
        slab = width * stripe
        running = state.reshape(4 * slab, LANES)
        panel = reversed_rows.reshape(4 * slab, LANES)
        own_basis = basis.reshape(4, width, width)
        own_values = eigval.reshape(4 * halves, LANES)
        vmem = pl.BlockSpec(memory_space=pltpu.VMEM)
        hbm = pl.BlockSpec(memory_space=pltpu.HBM)

        def blocks_shape(number, extra=0):
            return jax.ShapeDtypeStruct((number * width + extra, width), jnp.float32)

        def part(index):
            return slice(index * width, (index + 1) * width)

        def where_at(p, q, half):
            return pl.ds(p * slab + q * halves + half, width, stride=stripe)

        def joined(parts):
            return jnp.concatenate(parts, axis=1) if halves > 1 else parts[0]

        def read(ref, p, q):
            return joined([ref[where_at(p, q, half), :] for half in range(halves)])

        def write(ref, p, q, value):
            for half in range(halves):
                ref[where_at(p, q, half), :] = value[:, half * LANES : (half + 1) * LANES]

        def values_at(ref, p):
            return joined([ref[pl.ds(p * halves + half, 1), :] for half in range(halves)])

        def here():
            return lax.axis_index("row"), lax.axis_index("col")

        def near_row(d, c, q):
            return jnp.clip(local_row(d, c, q), 0, 3)

        def call(body, outputs, operands, specs=None, scratch=(), flops=0, seen=None):
            moved = sum(4 * int(np.prod(o.shape)) for o in (*operands, *outputs)) if seen is None else seen
            return pl.pallas_call(
                body,
                out_shape=outputs,
                in_specs=specs or [vmem] * len(operands),
                out_specs=[vmem] * len(outputs),
                scratch_shapes=scratch,
                compiler_params=pltpu.CompilerParams(vmem_limit_bytes=LIMIT),
                cost_estimate=pl.CostEstimate(flops=flops, bytes_accessed=moved, transcendentals=0),
            )(*operands)

        def slab_copy(ref, p, target, sem):
            return pltpu.make_async_copy(ref.at[pl.ds(pl.multiple_of(p * slab, slab), slab)], target, sem)

        def pack_first(state_ref, basis_ref, values_ref, own, upper, eigen, slabs, values, sems):
            r, c = here()
            column = jnp.where(c % rows == r, c, step(c, -1))
            index = column // rows
            copies = [
                slab_copy(state_ref, near_row(count - 1, c, q), slabs.at[q], sems.at[q]) for q in range(2)
            ]
            copies.append(pltpu.make_async_copy(basis_ref.at[index], eigen.at[pl.ds(0, width)], sems.at[2]))
            copies.append(pltpu.make_async_copy(values_ref, values, sems.at[3]))
            for copy in copies:
                copy.start()
            for target, q in ((own, 0), (upper, 1)):
                copies[q].wait()
                target[...] = read(slabs.at[q], 0, q)
            for copy in copies[2:]:
                copy.wait()
            eigen[width:, :] = jnp.broadcast_to(values_at(values, index), (8, width))

        def pack_second(state_ref, panel_ref, own, upper, often, rarely, slabs, panel_slabs, sems):
            r, c = here()
            places = [near_row(count, c, q) for q in range(2)]
            copies = [slab_copy(state_ref, places[q], slabs.at[q], sems.at[q]) for q in range(2)]
            copies.append(pltpu.make_async_copy(panel_ref, panel_slabs, sems.at[2]))
            for copy in copies:
                copy.start()
            for copy in copies:
                copy.wait()
            for target, q in ((own, 0), (upper, 1)):
                target[part(0), :] = read(slabs.at[q], 0, q)
                target[part(1), :] = read(panel_slabs, places[q], q)
            last = (r == rows - 1).astype(jnp.int32)
            for target, chosen in ((often, common), (rarely, seldom)):
                for index, (p, q) in enumerate(chosen):
                    target[part(index), :] = read(panel_slabs, jnp.maximum(p - last, 0), q)

        def column_of(values):
            return jnp.broadcast_to(values, (width, width)).T

        def solve(right_side, near, near_values, far_basis, far_values):
            inner = product(near.T, right_side)
            inner = product(inner, far_basis)
            inner = inner / (column_of(near_values) + far_values)
            return product(product(near, inner), far_basis, ((1,), (1,)))

        def solve_first(own, mirror, eigen, basis_ref, values_ref, out):
            r, c = here()
            mine = holds(count - 1, r, c)

            @pl.when(mine)
            def _():
                p = jnp.clip(solved_row(count - 1, c), 0, 3)
                right_side = own[...] + mirror[...].T
                near, values = basis_ref[p], values_at(values_ref, p)
                out[...] = solve(right_side, near, values, eigen[:width, :], eigen[width : width + 1, :])

            @pl.when(jnp.logical_not(mine))
            def _():
                out[...] = jnp.zeros_like(out)

        def solve_second(own, upper, mirror, eigen, left_ref, above_ref, basis_ref, values_ref, out):
            r, c = here()
            mine = holds(count, r, c)
            inside = within(r)
            lone = c == 0

            @pl.when(mine)
            def _():
                def own_part(index):
                    return jnp.where(lone, upper[part(index), :], own[part(index), :])

                def mirror_part(index):
                    return jnp.where(r == 0, upper[part(index), :], mirror[part(index), :])

                p = jnp.clip(solved_row(count, c), 0, 3)
                before = left_ref[...]
                turned = jnp.where(lone, before.T, above_ref[...])
                right_side = own_part(0) - product(before, own_part(1))
                right_side = right_side + (mirror_part(0).T - product(mirror_part(1).T, turned))
                index = (c + cols * lone) // rows
                far_basis = jnp.where(inside, basis_ref[index], eigen[:width, :])
                far_values = jnp.where(inside, values_at(values_ref, index), eigen[width : width + 1, :])
                out[...] = solve(right_side, basis_ref[p], values_at(values_ref, p), far_basis, far_values)

            @pl.when(jnp.logical_not(mine))
            def _():
                out[...] = jnp.zeros_like(out)

        def update(d, running, shares, sources, rows_of_a):
            arrays = []
            for share in shares:
                for array, _, _ in share:
                    if not any(array is other for other in arrays):
                        arrays.append(array)

            def body(running_ref, *refs):
                r, c = here()
                parts, given = refs[: len(arrays)], refs[len(arrays) : -2]
                out, blocks = refs[-2], refs[-1]
                for index, share in enumerate(shares):
                    total = None
                    residue = (d - r if index < 2 else r) % stride
                    for array, row, n in share:
                        ref = next(p for p, a in zip(parts, arrays) if a is array)
                        value = ref[part(row), :]
                        if n and d < count:
                            value = jnp.where((c - n) % stride == residue, value, 0.0)
                        total = value if total is None else total + value
                    blocks[index] = total
                for p in range(4):
                    k = p * rows + r
                    partner = d - k
                    source = jnp.minimum(k, partner) % cols
                    half = (c // stride - source // stride) % LINE // 2
                    turned = 2 * k < d
                    index = half + 2 * turned.astype(jnp.int32)
                    if d == count:
                        index = jnp.where(within(r), half, index)

                    def block():
                        found = blocks[index]
                        return jnp.where(turned, found.T, found) if p < 3 else found

                    for q in range(2):
                        at = q * cols + c
                        old = read(running_ref, p, q)
                        write(out, p, q, old)
                        a_block = rows_of_a(given, p, q)
                        if a_block is not None:

                            @pl.when((at > partner) & (partner < count))
                            def _():
                                write(out, p, q, old - product(block(), a_block()))

                        @pl.when(at == partner)
                        def _():
                            write(out, p, q, block())

            return call(
                body,
                [jax.ShapeDtypeStruct(running.shape, jnp.float32)],
                (running, *arrays, *sources),
                scratch=[pltpu.VMEM((4, width, width), jnp.float32)],
                flops=16 * width**3 * 6,
            )[0]

        def own_rows(given, p, q):
            return lambda: read(given[0], p, q)

        def next_rows(given, p, q):
            for ref, chosen in zip(given, (common, seldom)):
                if (p, q) in chosen:
                    index = chosen.index((p, q))
                    return lambda: ref[part(index), :]
            return None

        def spread(value, d, sources, direct, held=(), held_turned=()):
            shifts, shifts_turned, steps, steps_turned = spread_moves(d, sources, direct)
            moved = [value] + [send(value, moves) for moves in shifts[1:]]
            shares = [[(array, 0, 0) for array in moved[2 * half : 2 * half + 2]] for half in range(2)]
            if not direct:
                for half in range(2):
                    both = after(moved[2 * half] + moved[2 * half + 1], *held)
                    for n in range(1, stride):
                        shares[half].append((send(both, steps[half, n]), 0, n))
                pair = jnp.concatenate([sum(a for a, _, _ in share) for share in shares], axis=0)
                got = send(pair, across_moves(d, sources))
                return shares + [[(got, 0, 0)], [(got, 1, 0)]]
            low = after(value, *held_turned)
            low_moved = [send(low, moves) for moves in shifts_turned]
            shares += [[(array, 0, 0) for array in low_moved[2 * half : 2 * half + 2]] for half in range(2)]
            for half in range(2):
                both = after(moved[2 * half] + moved[2 * half + 1], *held)
                both_low = low_moved[2 * half] + low_moved[2 * half + 1]
                for n in range(1, stride):
                    if d < count:
                        got = send(both + both_low, steps[half, n] + steps_turned[half, n])
                        shares[half].append((got, 0, n))
                        shares[2 + half].append((got, 0, n))
                    else:
                        shares[half].append((send(both, steps[half, n]), 0, n))
                        shares[2 + half].append((send(both_low, steps_turned[half, n]), 0, n))
            return shares

        solve_flops = 4 * 2 * 6 * width**3

        own, upper, eigen = call(
            pack_first,
            [blocks_shape(1), blocks_shape(1), blocks_shape(1, 8)],
            (running, own_basis, own_values),
            specs=[hbm, hbm, hbm],
            scratch=[
                pltpu.VMEM((2, slab, LANES), jnp.float32),
                pltpu.VMEM((4 * halves, LANES), jnp.float32),
                pltpu.SemaphoreType.DMA((4,)),
            ],
            seen=PACK_SEEN,
        )
        mirror = send(upper, mirror_first)
        eigen = send(eigen, far)
        own_pair, upper_pair, often, rarely = call(
            pack_second,
            [blocks_shape(2), blocks_shape(2), blocks_shape(len(common)), blocks_shape(len(seldom))],
            (running, panel),
            specs=[hbm, hbm],
            scratch=[
                pltpu.VMEM((2, slab, LANES), jnp.float32),
                pltpu.VMEM((4 * slab, LANES), jnp.float32),
                pltpu.SemaphoreType.DMA((3,)),
            ],
            seen=PACK_SEEN,
        )
        pair_mirror = send(upper_pair, mirror_second)
        (solved,) = call(
            solve_first,
            [blocks_shape(1)],
            (own, mirror, eigen, own_basis, own_values),
            flops=solve_flops,
        )

        before = send(solved, left)
        above_it = send(solved, above)
        options = {"none": (), "solved": (solved,), "before": (before,), "direct": (before, above_it)}
        often = send(after(often, *options.get(GATE_PANEL, ())), panel_moves(common))
        rarely = send(after(rarely, *options.get(GATE_PANEL, ())), panel_moves(seldom))
        ready = {"none": (), "often": (often,), "both": (often, rarely)}[GATE_SOLVE]
        (solved_next,) = call(
            solve_second,
            [blocks_shape(1)],
            (after(own_pair, *ready), upper_pair, pair_mirror, eigen, before, above_it, own_basis, own_values),
            flops=3 * solve_flops // 2,
        )
        options["next"] = (solved_next,)
        options["often"], options["both"] = (often,), (often, rarely)
        shares = spread(
            after(solved, *options[GATE_SPREAD]),
            count - 1,
            first,
            DIRECT[0],
            options[GATE_FORWARD],
            options[GATE_LOW],
        )
        running = update(count - 1, running, shares, [panel], own_rows)

        shares = spread(solved_next, count, second, DIRECT[1])
        running = update(count, running, shares, [often, rarely], next_rows)
        return running.reshape(state.shape)

    placed = (
        P(None, "row", None, None, "col", None),
        P(None, "row", None, None, "col", None),
        P(None, "row", None, None),
        P(None, "row", None),
    )
    return jax.shard_map(
        local,
        mesh=mesh,
        in_specs=placed,
        out_specs=P(None, "row", None, None, "col", None),
        check_vma=False,
    )
```

```python
import numpy as np
import jax
import jax.numpy as jnp
from jax import lax
from jax.experimental import pallas as pl
from jax.experimental.pallas import tpu as pltpu
from jax.sharding import PartitionSpec as P

AXES = ("row", "col")
LANES = 128
LIMIT = 40 * 1024 * 1024
LINE = 4
GATE_SPREAD = "none"
GATE_PANEL = "solved"
GATE_FORWARD = "none"
GATE_SOLVE = "none"
GATE_LOW = "none"
GATE_SECOND = ("own","often")


def product(first, second, dims=((1,), (0,))):
    return lax.dot_general(
        first,
        second,
        (dims, ((), ())),
        precision=lax.Precision.HIGHEST,
        preferred_element_type=jnp.float32,
    )


def solution(mesh):
    rows, cols = mesh.shape["row"], mesh.shape["col"]
    count = 4 * rows
    assert cols == 2 * rows and cols % LINE == 0
    stride = cols // LINE
    devices = [(r, c) for r in range(rows) for c in range(cols)]

    def holds(d, r, c):
        return c % rows == (d - r) % rows

    def local_row(d, c, q):
        return (d - q * cols - c) // rows

    def within(r):
        return r % (rows // 2) == 0

    def shift(c, by):
        return (c + by * stride) % cols

    def step(c, by):
        return c // stride * stride + (c + by) % stride

    first = [device for device in devices if holds(count - 1, *device)]
    second = [device for device in devices if holds(count, *device)]

    def send(value, moves):
        assert len({s for s, _ in moves}) == len(moves) == len({t for _, t in moves})
        return lax.ppermute(value, AXES, [(s[0] * cols + s[1], t[0] * cols + t[1]) for s, t in moves])

    def after(value, *others):
        return lax.optimization_barrier((value, *others))[0] if others else value

    mirror_first = [((rows - 1 - r, cols - 1 - c), (r, c)) for r, c in first]
    mirror_second = [((-r % rows, -c % cols), (r, c)) for r, c in second if r != 0]
    far = [((c % rows, c), (r, c)) for r, c in first]
    far += [((c % rows, step(c, 1)), (r, c)) for r, c in second if not within(r)]
    left = [((r, (c - 1) % cols), (r, c)) for r, c in second]
    above = [(((r - 1) % rows, c), (r, c)) for r, c in second]

    def middle(d, c):
        return (c == 0) & (d == count)

    def solved_row(d, c):
        return local_row(d, c, 0) - 2 * middle(d, c)

    def wants(k, d, c):
        return 0 <= d - k < count and cols + c >= d - k

    def needs(d, source):
        r, c = source
        k = solved_row(d, c) * rows + r
        at_all = range(cols)
        if d == count and within(r):
            return {(r, at) for at in at_all if wants(k, d, at) or wants(d - k, d, at)}
        return {(r, at) for at in at_all if wants(k, d, at)}

    def needs_turned(d, source):
        r, c = source
        if d == count and within(r):
            return set()
        k = d - (solved_row(d, c) * rows + r)
        return {(k % rows, at) for at in range(cols) if wants(k, d, at)}

    def spread_moves(d, sources):
        own, turned = {}, {}
        for source in sources:
            own[source], turned[source] = needs(d, source), needs_turned(d, source)
            if d == count:
                own[source] = own[source] | {(source[0], at) for _, at in turned[source]}

        def in_group(used, r, at):
            return any((r, step(at, n)) in used for n in range(stride))

        shifts, across = [], set()
        steps, steps_turned = ({n: set() for n in range(1, stride)} for _ in range(2))
        for by in range(LINE):
            moves = []
            for r, c in sources:
                at, other = shift(c, by), (d - r) % rows
                here, there = in_group(own[r, c], r, at), in_group(turned[r, c], other, at)
                if here or (d < count and there):
                    moves.append(((r, c), (r, at)))
                if d < count and there:
                    across.add(((r, at), (other, at)))
                for n in range(1, stride):
                    near = step(at, n)
                    if (r, near) in own[r, c]:
                        steps[n].add(((r, at), (r, near)))
                    if d < count and (other, near) in turned[r, c]:
                        steps_turned[n].add(((other, at), (other, near)))
            shifts.append(moves)
        if d == count:
            targets = set().union(*turned.values())
            across = {(((d - t) % rows, c), (t, c)) for t, c in targets}
        return shifts[1:], steps, steps_turned, sorted(across)

    def reached(device, p, q):
        k = p * rows + device[0]
        return 0 < k and q * cols + device[1] > count - k

    slots = [(p, q) for p in range(4) for q in range(2)]
    common = [s for s in slots if reached((rows // 2, cols // 2), *s)]
    seldom = [s for s in slots if s not in common and any(reached(device, *s) for device in devices)]

    def panel_moves(chosen):
        return [
            (((r - 1) % rows, c), (r, c)) for r, c in devices if any(reached((r, c), *s) for s in chosen)
        ]

    def local(reversed_rows, state, basis, eigval):
        width = state.shape[2]
        halves = width // LANES
        stripe = 2 * halves
        slab = width * stripe
        running = state.reshape(4 * slab, LANES)
        panel = reversed_rows.reshape(4 * slab, LANES)
        own_basis = basis.reshape(4, width, width)
        own_values = eigval.reshape(4 * halves, LANES)
        vmem = pl.BlockSpec(memory_space=pltpu.VMEM)
        hbm = pl.BlockSpec(memory_space=pltpu.HBM)

        def blocks_shape(number, extra=0):
            return jax.ShapeDtypeStruct((number * width + extra, width), jnp.float32)

        def part(index):
            return slice(index * width, (index + 1) * width)

        def where_at(p, q, half):
            return pl.ds(p * slab + q * halves + half, width, stride=stripe)

        def joined(parts):
            return jnp.concatenate(parts, axis=1) if halves > 1 else parts[0]

        def read(ref, p, q):
            return joined([ref[where_at(p, q, half), :] for half in range(halves)])

        def write(ref, p, q, value):
            for half in range(halves):
                ref[where_at(p, q, half), :] = value[:, half * LANES : (half + 1) * LANES]

        def values_at(ref, p):
            return joined([ref[pl.ds(p * halves + half, 1), :] for half in range(halves)])

        def here():
            return lax.axis_index("row"), lax.axis_index("col")

        def near_row(d, c, q):
            return jnp.clip(local_row(d, c, q), 0, 3)

        def call(body, outputs, operands, specs=None, scratch=(), flops=0):
            moved = sum(4 * int(np.prod(o.shape)) for o in (*operands, *outputs))
            return pl.pallas_call(
                body,
                out_shape=outputs,
                in_specs=specs or [vmem] * len(operands),
                out_specs=[vmem] * len(outputs),
                scratch_shapes=scratch,
                compiler_params=pltpu.CompilerParams(vmem_limit_bytes=LIMIT),
                cost_estimate=pl.CostEstimate(flops=flops, bytes_accessed=moved, transcendentals=0),
            )(*operands)

        def slab_copy(ref, p, target, sem):
            return pltpu.make_async_copy(ref.at[pl.ds(pl.multiple_of(p * slab, slab), slab)], target, sem)

        def pack_first(state_ref, basis_ref, values_ref, own, upper, eigen, slabs, values, sems):
            r, c = here()
            column = jnp.where(c % rows == r, c, step(c, -1))
            index = column // rows
            copies = [
                slab_copy(state_ref, near_row(count - 1, c, q), slabs.at[q], sems.at[q]) for q in range(2)
            ]
            copies.append(pltpu.make_async_copy(basis_ref.at[index], eigen.at[pl.ds(0, width)], sems.at[2]))
            copies.append(pltpu.make_async_copy(values_ref, values, sems.at[3]))
            for copy in copies:
                copy.start()
            for target, q in ((own, 0), (upper, 1)):
                copies[q].wait()
                target[...] = read(slabs.at[q], 0, q)
            for copy in copies[2:]:
                copy.wait()
            eigen[width:, :] = jnp.broadcast_to(values_at(values, index), (8, width))

        def pack_second(state_ref, panel_ref, own, upper, often, rarely, slabs, panel_slabs, sems):
            r, c = here()
            places = [near_row(count, c, q) for q in range(2)]
            copies = [slab_copy(state_ref, places[q], slabs.at[q], sems.at[q]) for q in range(2)]
            copies.append(pltpu.make_async_copy(panel_ref, panel_slabs, sems.at[2]))
            for copy in copies:
                copy.start()
            for copy in copies:
                copy.wait()
            for target, q in ((own, 0), (upper, 1)):
                target[part(0), :] = read(slabs.at[q], 0, q)
                target[part(1), :] = read(panel_slabs, places[q], q)
            last = (r == rows - 1).astype(jnp.int32)
            for target, chosen in ((often, common), (rarely, seldom)):
                for index, (p, q) in enumerate(chosen):
                    target[part(index), :] = read(panel_slabs, jnp.maximum(p - last, 0), q)

        def column_of(values):
            return jnp.broadcast_to(values, (width, width)).T

        def solve(right_side, near, near_values, far_basis, far_values):
            inner = product(near.T, right_side)
            inner = product(inner, far_basis)
            inner = inner / (column_of(near_values) + far_values)
            return product(product(near, inner), far_basis, ((1,), (1,)))

        def solve_first(own, mirror, eigen, basis_ref, values_ref, out):
            r, c = here()
            mine = holds(count - 1, r, c)

            @pl.when(mine)
            def _():
                p = jnp.clip(solved_row(count - 1, c), 0, 3)
                right_side = own[...] + mirror[...].T
                near, values = basis_ref[p], values_at(values_ref, p)
                out[...] = solve(right_side, near, values, eigen[:width, :], eigen[width : width + 1, :])

            @pl.when(jnp.logical_not(mine))
            def _():
                out[...] = jnp.zeros_like(out)

        def solve_second(own, upper, mirror, eigen, left_ref, above_ref, basis_ref, values_ref, out):
            r, c = here()
            mine = holds(count, r, c)
            inside = within(r)
            lone = c == 0

            @pl.when(mine)
            def _():
                def own_part(index):
                    return jnp.where(lone, upper[part(index), :], own[part(index), :])

                def mirror_part(index):
                    return jnp.where(r == 0, upper[part(index), :], mirror[part(index), :])

                p = jnp.clip(solved_row(count, c), 0, 3)
                before = left_ref[...]
                turned = jnp.where(lone, before.T, above_ref[...])
                right_side = own_part(0) - product(before, own_part(1))
                right_side = right_side + (mirror_part(0).T - product(mirror_part(1).T, turned))
                index = (c + cols * lone) // rows
                far_basis = jnp.where(inside, basis_ref[index], eigen[:width, :])
                far_values = jnp.where(inside, values_at(values_ref, index), eigen[width : width + 1, :])
                out[...] = solve(right_side, basis_ref[p], values_at(values_ref, p), far_basis, far_values)

            @pl.when(jnp.logical_not(mine))
            def _():
                out[...] = jnp.zeros_like(out)

        def block_sum(refs, half):
            total = refs[0][part(half), :]
            for ref in refs[1:]:
                total = total + ref[part(half), :]
            return total

        def half_of(r, c, d, k):
            source = jnp.minimum(k, d - k) % cols
            return (c // stride - source // stride) % LINE // 2

        def update(running, panel, spread_first, spread_second, sources):
            own_first, low_first, steps_first, steps_low = spread_first
            own_second, steps_second = spread_second
            operands = (
                running, panel, own_first, *steps_first, low_first, *steps_low, own_second, *steps_second,
                *sources,
            )

            def body(running_ref, panel_ref, *refs):
                r, c = here()
                first_refs, low_refs = refs[:stride], refs[stride : 2 * stride]
                second_refs, refs = refs[2 * stride : 3 * stride], refs[3 * stride :]
                given, out, blocks = refs[: len(sources)], refs[len(sources)], refs[len(sources) + 1]
                for half in range(2):
                    blocks[half] = block_sum(first_refs, half)
                    blocks[2 + half] = block_sum(low_refs, half)
                    blocks[4 + half] = block_sum(second_refs, half)
                inside = within(r)
                for p in range(4):
                    k = p * rows + r
                    partner = count - 1 - k

                    def block_first():
                        found = blocks[half_of(r, c, count - 1, k) + (2 if p < 2 else 0)]
                        return found.T if p < 2 else found

                    def block_second():
                        found = blocks[4 + half_of(r, c, count, k)]
                        return found.T if p < 2 else found

                    for q in range(2):
                        at = q * cols + c
                        old = read(running_ref, p, q)
                        write(out, p, q, old)
                        if p < 2 and q == 0:
                            continue
                        a_second = next_rows(given, p, q)

                        @pl.when(at == partner)
                        def _():
                            write(out, p, q, block_first())

                        known = inside if p < 2 else at == at

                        @pl.when((at == partner + 1) & known)
                        def _():
                            write(out, p, q, block_second())

                        if a_second is None:
                            continue

                        @pl.when((at > partner + 1) & known)
                        def _():
                            change = product(block_first(), read(panel_ref, p, q))
                            change = change + product(block_second(), a_second())
                            write(out, p, q, old - change)

                        if p < 2:

                            @pl.when((at > partner + 1) & jnp.logical_not(known))
                            def _():
                                write(out, p, q, old - product(block_first(), read(panel_ref, p, q)))

            return call(
                body,
                [jax.ShapeDtypeStruct(running.shape, jnp.float32)],
                operands,
                scratch=[pltpu.VMEM((6, width, width), jnp.float32)],
                flops=16 * width**3 * 6,
            )[0]

        def finish(running, low, sources):
            def body(running_ref, low_ref, *refs):
                given, out, slabs, sems = refs[: len(sources)], refs[-3], refs[-2], refs[-1]
                r, c = here()
                at = cols + c
                del running_ref

                def touched(p):
                    return jnp.logical_not(within(r)) & (at >= count - (p * rows + r))

                for p in range(2):

                    @pl.when(touched(p))
                    def _():
                        pltpu.make_async_copy(out.at[pl.ds(p * slab, slab)], slabs.at[p], sems.at[p]).start()

                for p in range(2):
                    k = p * rows + r

                    @pl.when(touched(p))
                    def _():
                        pltpu.make_async_copy(out.at[pl.ds(p * slab, slab)], slabs.at[p], sems.at[p]).wait()
                        start = pl.multiple_of(half_of(r, c, count, k) * width, width)
                        block = low_ref[pl.ds(start, width), :].T
                        a_block = next_rows(given, p, 1)

                        @pl.when(at == count - k)
                        def _():
                            write(slabs.at[p], 0, 1, block)

                        @pl.when(at > count - k)
                        def _():
                            write(slabs.at[p], 0, 1, read(slabs.at[p], 0, 1) - product(block, a_block()))

                        pltpu.make_async_copy(slabs.at[p], out.at[pl.ds(p * slab, slab)], sems.at[p]).start()

                for p in range(2):

                    @pl.when(touched(p))
                    def _():
                        pltpu.make_async_copy(slabs.at[p], out.at[pl.ds(p * slab, slab)], sems.at[p]).wait()

            return pl.pallas_call(
                body,
                out_shape=jax.ShapeDtypeStruct(running.shape, jnp.float32),
                in_specs=[hbm] + [vmem] * (1 + len(sources)),
                out_specs=hbm,
                scratch_shapes=[pltpu.VMEM((2, slab, LANES), jnp.float32), pltpu.SemaphoreType.DMA((2,))],
                input_output_aliases={0: 0},
                compiler_params=pltpu.CompilerParams(vmem_limit_bytes=LIMIT),
                cost_estimate=pl.CostEstimate(
                    flops=2 * width**3 * 12, bytes_accessed=4 * slab * LANES * 4, transcendentals=0
                ),
            )(running, low, *sources)

        def next_rows(given, p, q):
            for ref, chosen in zip(given, (common, seldom)):
                if (p, q) in chosen:
                    index = chosen.index((p, q))
                    return lambda: ref[part(index), :]
            return None

        def spread(value, d, sources, held=(), held_low=()):
            shifts, steps, steps_turned, across = spread_moves(d, sources)
            moved = [value] + [send(value, moves) for moves in shifts]
            pair = jnp.concatenate([moved[0] + moved[1], moved[2] + moved[3]], axis=0)
            pair = after(pair, *held)
            got = [send(pair, sorted(steps[n])) for n in range(1, stride)]
            if d < count:
                low = send(after(pair, *held_low), across)
                return pair, low, got, [send(low, sorted(steps_turned[n])) for n in range(1, stride)]
            return pair, got, send(sum(got, pair), across)

        def in_hbm(*arrays):
            return tuple(pltpu.with_memory_space_constraint(array, pltpu.HBM) for array in arrays)

        solve_flops = 4 * 2 * 6 * width**3

        own, upper, eigen = call(
            pack_first,
            [blocks_shape(1), blocks_shape(1), blocks_shape(1, 8)],
            in_hbm(running, own_basis, own_values),
            specs=[hbm, hbm, hbm],
            scratch=[
                pltpu.VMEM((2, slab, LANES), jnp.float32),
                pltpu.VMEM((4 * halves, LANES), jnp.float32),
                pltpu.SemaphoreType.DMA((4,)),
            ],
        )
        mirror = send(upper, mirror_first)
        eigen = send(eigen, far)
        own_pair, upper_pair, often, rarely = call(
            pack_second,
            [blocks_shape(2), blocks_shape(2), blocks_shape(len(common)), blocks_shape(len(seldom))],
            in_hbm(after(running, own), panel),
            specs=[hbm, hbm],
            scratch=[
                pltpu.VMEM((2, slab, LANES), jnp.float32),
                pltpu.VMEM((4 * slab, LANES), jnp.float32),
                pltpu.SemaphoreType.DMA((3,)),
            ],
        )
        pair_mirror = send(upper_pair, mirror_second)
        (solved,) = call(
            solve_first,
            [blocks_shape(1)],
            (own, mirror, eigen, own_basis, own_values),
            flops=solve_flops,
        )

        before = send(solved, left)
        above_it = send(solved, above)
        options = {"none": (), "solved": (solved,), "before": (before,), "direct": (before, above_it)}
        often = send(after(often, *options.get(GATE_PANEL, ())), panel_moves(common))
        rarely = send(after(rarely, *options.get(GATE_PANEL, ())), panel_moves(seldom))
        ready = {"none": (), "often": (often,), "both": (often, rarely)}[GATE_SOLVE]
        (solved_next,) = call(
            solve_second,
            [blocks_shape(1)],
            (after(own_pair, *ready), upper_pair, pair_mirror, eigen, before, above_it, own_basis, own_values),
            flops=3 * solve_flops // 2,
        )
        options["next"] = (solved_next,)
        options["often"], options["both"] = (often,), (often, rarely)
        spread_first = spread(
            after(solved, *options[GATE_SPREAD]), count - 1, first, options[GATE_FORWARD], options[GATE_LOW]
        )
        pair, low, got, got_low = spread_first
        earlier = {"often": often, "rarely": rarely, "own": got[0], "low": low, "turned": got_low[0]}
        *spread_second, low = spread(solved_next, count, second, [earlier[name] for name in GATE_SECOND])
        running = update(running, panel, spread_first, spread_second, [often, rarely])
        running = finish(running, low, [often, rarely])
        return running.reshape(state.shape)

    placed = (
        P(None, "row", None, None, "col", None),
        P(None, "row", None, None, "col", None),
        P(None, "row", None, None),
        P(None, "row", None),
    )
    return jax.shard_map(
        local,
        mesh=mesh,
        in_specs=placed,
        out_specs=P(None, "row", None, None, "col", None),
        check_vma=False,
    )
```

```python
import numpy as np
import jax
import jax.numpy as jnp
from jax import lax
from jax.experimental import pallas as pl
from jax.experimental.pallas import tpu as pltpu
from jax.sharding import PartitionSpec as P

AXES = ("row", "col")
LANES = 128
LIMIT = 40 * 1024 * 1024
LINE = 4
GATE_SPREAD = "none"
GATE_PANEL = "solved"
GATE_FORWARD = "none"
GATE_SOLVE = "none"
GATE_LOW = "none"
GATE_SECOND = ("own", "often")
PACK_EARLY = True
ONE_PANEL = False


def product(first, second, dims=((1,), (0,))):
    return lax.dot_general(
        first,
        second,
        (dims, ((), ())),
        precision=lax.Precision.HIGHEST,
        preferred_element_type=jnp.float32,
    )


def quick_product(first, second):
    parts = []
    for value in (first, second):
        high = value.astype(jnp.bfloat16)
        parts.append((high, (value - high.astype(jnp.float32)).astype(jnp.bfloat16)))
    (high, low), (other_high, other_low) = parts

    def one_pass(a, b):
        return jnp.dot(a, b, preferred_element_type=jnp.float32)

    return one_pass(high, other_high) + (one_pass(high, other_low) + one_pass(low, other_high))


def solution(mesh):
    rows, cols = mesh.shape["row"], mesh.shape["col"]
    count = 4 * rows
    assert cols == 2 * rows and cols % LINE == 0
    stride = cols // LINE
    devices = [(r, c) for r in range(rows) for c in range(cols)]

    def holds(d, r, c):
        return c % rows == (d - r) % rows

    def local_row(d, c, q):
        return (d - q * cols - c) // rows

    def within(r):
        return r % (rows // 2) == 0

    def shift(c, by):
        return (c + by * stride) % cols

    def step(c, by):
        return c // stride * stride + (c + by) % stride

    first = [device for device in devices if holds(count - 1, *device)]
    second = [device for device in devices if holds(count, *device)]

    def send(value, moves):
        assert len({s for s, _ in moves}) == len(moves) == len({t for _, t in moves})
        return lax.ppermute(value, AXES, [(s[0] * cols + s[1], t[0] * cols + t[1]) for s, t in moves])

    def after(value, *others):
        return lax.optimization_barrier((value, *others))[0] if others else value

    mirror_first = [((rows - 1 - r, cols - 1 - c), (r, c)) for r, c in first]
    mirror_second = [((-r % rows, -c % cols), (r, c)) for r, c in second if r != 0]
    far = [((c % rows, c), (r, c)) for r, c in first]
    far += [((c % rows, step(c, 1)), (r, c)) for r, c in second if not within(r)]
    left = [((r, (c - 1) % cols), (r, c)) for r, c in second]
    above = [(((r - 1) % rows, c), (r, c)) for r, c in second]

    def middle(d, c):
        return (c == 0) & (d == count)

    def solved_row(d, c):
        return local_row(d, c, 0) - 2 * middle(d, c)

    def wants(k, d, c):
        return 0 <= d - k < count and cols + c >= d - k

    def needs(d, source):
        r, c = source
        k = solved_row(d, c) * rows + r
        at_all = range(cols)
        if d == count and within(r):
            return {(r, at) for at in at_all if wants(k, d, at) or wants(d - k, d, at)}
        return {(r, at) for at in at_all if wants(k, d, at)}

    def needs_turned(d, source):
        r, c = source
        if d == count and within(r):
            return set()
        k = d - (solved_row(d, c) * rows + r)
        return {(k % rows, at) for at in range(cols) if wants(k, d, at)}

    def spread_moves(d, sources):
        own, turned = {}, {}
        for source in sources:
            own[source], turned[source] = needs(d, source), needs_turned(d, source)
            if d == count:
                own[source] = own[source] | {(source[0], at) for _, at in turned[source]}

        def in_group(used, r, at):
            return any((r, step(at, n)) in used for n in range(stride))

        shifts, across = [], set()
        steps, steps_turned = ({n: set() for n in range(1, stride)} for _ in range(2))
        for by in range(LINE):
            moves = []
            for r, c in sources:
                at, other = shift(c, by), (d - r) % rows
                here, there = in_group(own[r, c], r, at), in_group(turned[r, c], other, at)
                if here or (d < count and there):
                    moves.append(((r, c), (r, at)))
                if d < count and there:
                    across.add(((r, at), (other, at)))
                for n in range(1, stride):
                    near = step(at, n)
                    if (r, near) in own[r, c]:
                        steps[n].add(((r, at), (r, near)))
                    if d < count and (other, near) in turned[r, c]:
                        steps_turned[n].add(((other, at), (other, near)))
            shifts.append(moves)
        if d == count:
            targets = set().union(*turned.values())
            across = {(((d - t) % rows, c), (t, c)) for t, c in targets}
        return shifts[1:], steps, steps_turned, sorted(across)

    def reached(device, p, q):
        k = p * rows + device[0]
        return 0 < k and q * cols + device[1] > count - k

    slots = [(p, q) for p in range(4) for q in range(2)]
    common = [s for s in slots if reached((rows // 2, cols // 2), *s)]
    if ONE_PANEL:
        common = [s for s in slots if any(reached(device, *s) for device in devices)]
    seldom = [s for s in slots if s not in common and any(reached(device, *s) for device in devices)]

    messages = [chosen for chosen in (common, seldom) if chosen]

    def panel_moves(chosen):
        return [
            (((r - 1) % rows, c), (r, c)) for r, c in devices if any(reached((r, c), *s) for s in chosen)
        ]

    def local(reversed_rows, state, basis, eigval):
        width = state.shape[2]
        halves = width // LANES
        stripe = 2 * halves
        slab = width * stripe
        running = state.reshape(4 * slab, LANES)
        panel = reversed_rows.reshape(4 * slab, LANES)
        own_basis = basis.reshape(4, width, width)
        own_values = eigval.reshape(4 * halves, LANES)
        vmem = pl.BlockSpec(memory_space=pltpu.VMEM)
        hbm = pl.BlockSpec(memory_space=pltpu.HBM)

        def blocks_shape(number, extra=0):
            return jax.ShapeDtypeStruct((number * width + extra, width), jnp.float32)

        def part(index):
            return slice(index * width, (index + 1) * width)

        def where_at(p, q, half):
            return pl.ds(p * slab + q * halves + half, width, stride=stripe)

        def joined(parts):
            return jnp.concatenate(parts, axis=1) if halves > 1 else parts[0]

        def read(ref, p, q):
            return joined([ref[where_at(p, q, half), :] for half in range(halves)])

        def write(ref, p, q, value):
            for half in range(halves):
                ref[where_at(p, q, half), :] = value[:, half * LANES : (half + 1) * LANES]

        def values_at(ref, p):
            return joined([ref[pl.ds(p * halves + half, 1), :] for half in range(halves)])

        def here():
            return lax.axis_index("row"), lax.axis_index("col")

        def near_row(d, c, q):
            return jnp.clip(local_row(d, c, q), 0, 3)

        def call(body, outputs, operands, specs=None, scratch=(), flops=0):
            moved = sum(4 * int(np.prod(o.shape)) for o in (*operands, *outputs))
            return pl.pallas_call(
                body,
                out_shape=outputs,
                in_specs=specs or [vmem] * len(operands),
                out_specs=[vmem] * len(outputs),
                scratch_shapes=scratch,
                compiler_params=pltpu.CompilerParams(vmem_limit_bytes=LIMIT),
                cost_estimate=pl.CostEstimate(flops=flops, bytes_accessed=moved, transcendentals=0),
            )(*operands)

        def slab_copy(ref, p, target, sem):
            return pltpu.make_async_copy(ref.at[pl.ds(pl.multiple_of(p * slab, slab), slab)], target, sem)

        def pack_first(state_ref, basis_ref, values_ref, own, upper, eigen, slabs, values, sems):
            r, c = here()
            column = jnp.where(c % rows == r, c, step(c, -1))
            index = column // rows
            copies = [
                slab_copy(state_ref, near_row(count - 1, c, q), slabs.at[q], sems.at[q]) for q in range(2)
            ]
            copies.append(pltpu.make_async_copy(basis_ref.at[index], eigen.at[pl.ds(0, width)], sems.at[2]))
            copies.append(pltpu.make_async_copy(values_ref, values, sems.at[3]))
            for copy in copies:
                copy.start()
            for target, q in ((own, 0), (upper, 1)):
                copies[q].wait()
                target[...] = read(slabs.at[q], 0, q)
            for copy in copies[2:]:
                copy.wait()
            eigen[width:, :] = jnp.broadcast_to(values_at(values, index), (8, width))

        def pack_second(state_ref, panel_ref, own, upper, *refs):
            targets, (slabs, panel_slabs, sems) = refs[:-3], refs[-3:]
            r, c = here()
            places = [near_row(count, c, q) for q in range(2)]
            copies = [slab_copy(state_ref, places[q], slabs.at[q], sems.at[q]) for q in range(2)]
            copies.append(pltpu.make_async_copy(panel_ref, panel_slabs, sems.at[2]))
            for copy in copies:
                copy.start()
            for copy in copies:
                copy.wait()
            for target, q in ((own, 0), (upper, 1)):
                target[part(0), :] = read(slabs.at[q], 0, q)
                target[part(1), :] = read(panel_slabs, places[q], q)
            last = (r == rows - 1).astype(jnp.int32)
            for target, chosen in zip(targets, messages):
                for index, (p, q) in enumerate(chosen):
                    target[part(index), :] = read(panel_slabs, jnp.maximum(p - last, 0), q)

        def column_of(values):
            return jnp.broadcast_to(values, (width, width)).T

        def solve(right_side, near, near_values, far_basis, far_values):
            inner = product(near.T, right_side)
            inner = product(inner, far_basis)
            inner = inner / (column_of(near_values) + far_values)
            return product(product(near, inner), far_basis, ((1,), (1,)))

        def solve_first(own, mirror, eigen, basis_ref, values_ref, out):
            r, c = here()
            mine = holds(count - 1, r, c)

            @pl.when(mine)
            def _():
                p = jnp.clip(solved_row(count - 1, c), 0, 3)
                right_side = own[...] + mirror[...].T
                near, values = basis_ref[p], values_at(values_ref, p)
                out[...] = solve(right_side, near, values, eigen[:width, :], eigen[width : width + 1, :])

            @pl.when(jnp.logical_not(mine))
            def _():
                out[...] = jnp.zeros_like(out)

        def solve_second(own, upper, mirror, eigen, left_ref, above_ref, basis_ref, values_ref, out):
            r, c = here()
            mine = holds(count, r, c)
            inside = within(r)
            lone = c == 0

            @pl.when(mine)
            def _():
                def own_part(index):
                    return jnp.where(lone, upper[part(index), :], own[part(index), :])

                def mirror_part(index):
                    return jnp.where(r == 0, upper[part(index), :], mirror[part(index), :])

                p = jnp.clip(solved_row(count, c), 0, 3)
                before = left_ref[...]
                turned = jnp.where(lone, before.T, above_ref[...])
                right_side = own_part(0) - product(before, own_part(1))
                right_side = right_side + (mirror_part(0).T - product(mirror_part(1).T, turned))
                index = (c + cols * lone) // rows
                far_basis = jnp.where(inside, basis_ref[index], eigen[:width, :])
                far_values = jnp.where(inside, values_at(values_ref, index), eigen[width : width + 1, :])
                out[...] = solve(right_side, basis_ref[p], values_at(values_ref, p), far_basis, far_values)

            @pl.when(jnp.logical_not(mine))
            def _():
                out[...] = jnp.zeros_like(out)

        def half_of(r, c, d, k):
            source = jnp.minimum(k, d - k) % cols
            return (c // stride - source // stride) % LINE // 2

        def block_at(refs, half):
            where = pl.ds(pl.multiple_of(half * width, width), width)
            return sum((ref[where, :] for ref in refs[1:]), refs[0][where, :])

        def settle(p, q, old, first_block, second_block, a_first, a_second, store):
            r, c = here()
            at, partner = q * cols + c, count - 1 - (p * rows + r)

            @pl.when(at == partner)
            def _():
                store(first_block())

            @pl.when(at == partner + 1)
            def _():
                store(second_block())

            if a_second is not None:

                @pl.when(at > partner + 1)
                def _():
                    change = quick_product(first_block(), a_first())
                    store(old() - (change + quick_product(second_block(), a_second())))

        def update(running, panel, own_first, own_second, sources):
            def body(running_ref, panel_ref, *refs):
                r, c = here()
                first_refs, second_refs, given = refs[:stride], refs[stride : 2 * stride], refs[2 * stride : -1]
                out = refs[-1]
                out[: 2 * slab, :] = running_ref[: 2 * slab, :]
                for p in (2, 3):
                    k = p * rows + r
                    for q in range(2):
                        write(out, p, q, read(running_ref, p, q))
                        settle(
                            p,
                            q,
                            lambda: read(running_ref, p, q),
                            lambda: block_at(first_refs, half_of(r, c, count - 1, k)),
                            lambda: block_at(second_refs, half_of(r, c, count, k)),
                            lambda: read(panel_ref, p, q),
                            next_rows(given, p, q),
                            lambda value: write(out, p, q, value),
                        )

            return call(
                body,
                [jax.ShapeDtypeStruct(running.shape, jnp.float32)],
                (running, panel, *own_first, *own_second, *sources),
                flops=16 * width**3 * 6,
            )[0]

        def finish(running, panel, low_first, own_second, low_second, sources):
            def body(running_ref, panel_ref, *refs):
                del running_ref
                r, c = here()
                first_refs, second_refs = refs[:stride], refs[stride : 2 * stride]
                turned_ref, given = refs[2 * stride], refs[2 * stride + 1 : -3]
                out, slabs, sems = refs[-3:]
                at = cols + c

                def touched(p):
                    return at >= count - 1 - (p * rows + r)

                def slab_in(p):
                    return pltpu.make_async_copy(out.at[pl.ds(p * slab, slab)], slabs.at[p], sems.at[p])

                def slab_out(p):
                    return pltpu.make_async_copy(slabs.at[p], out.at[pl.ds(p * slab, slab)], sems.at[p])

                for p in range(2):

                    @pl.when(touched(p))
                    def _():
                        slab_in(p).start()

                for p in range(2):
                    k = p * rows + r

                    def second_block():
                        half = half_of(r, c, count, k)
                        own = block_at(second_refs, half)
                        return jnp.where(within(r), own, block_at((turned_ref,), half)).T

                    @pl.when(touched(p))
                    def _():
                        slab_in(p).wait()
                        settle(
                            p,
                            1,
                            lambda: read(slabs.at[p], 0, 1),
                            lambda: block_at(first_refs, half_of(r, c, count - 1, k)).T,
                            second_block,
                            lambda: read(panel_ref, p, 1),
                            next_rows(given, p, 1),
                            lambda value: write(slabs.at[p], 0, 1, value),
                        )
                        slab_out(p).start()

                for p in range(2):

                    @pl.when(touched(p))
                    def _():
                        slab_out(p).wait()

            operands = (running, panel, *low_first, *own_second, low_second, *sources)
            return pl.pallas_call(
                body,
                out_shape=jax.ShapeDtypeStruct(running.shape, jnp.float32),
                in_specs=[hbm] + [vmem] * (len(operands) - 1),
                out_specs=hbm,
                scratch_shapes=[pltpu.VMEM((2, slab, LANES), jnp.float32), pltpu.SemaphoreType.DMA((2,))],
                input_output_aliases={0: 0},
                compiler_params=pltpu.CompilerParams(vmem_limit_bytes=LIMIT),
                cost_estimate=pl.CostEstimate(
                    flops=2 * width**3 * 12, bytes_accessed=4 * slab * LANES * 4, transcendentals=0
                ),
            )(*operands)

        def next_rows(given, p, q):
            for ref, chosen in zip(given, messages):
                if (p, q) in chosen:
                    index = chosen.index((p, q))
                    return lambda: ref[part(index), :]
            return None

        def spread(value, d, sources, held=(), held_low=()):
            shifts, steps, steps_turned, across = spread_moves(d, sources)
            moved = [value] + [send(value, moves) for moves in shifts]
            pair = jnp.concatenate([moved[0] + moved[1], moved[2] + moved[3]], axis=0)
            pair = after(pair, *held)
            got = [send(pair, sorted(steps[n])) for n in range(1, stride)]
            if d < count:
                low = send(after(pair, *held_low), across)
                return pair, low, got, [send(low, sorted(steps_turned[n])) for n in range(1, stride)]
            return pair, got, send(sum(got, pair), across)

        def in_hbm(*arrays):
            return tuple(pltpu.with_memory_space_constraint(array, pltpu.HBM) for array in arrays)

        solve_flops = 4 * 2 * 6 * width**3

        own, upper, eigen = call(
            pack_first,
            [blocks_shape(1), blocks_shape(1), blocks_shape(1, 8)],
            in_hbm(running, own_basis, own_values),
            specs=[hbm, hbm, hbm],
            scratch=[
                pltpu.VMEM((2, slab, LANES), jnp.float32),
                pltpu.VMEM((4 * halves, LANES), jnp.float32),
                pltpu.SemaphoreType.DMA((4,)),
            ],
        )
        mirror = send(upper, mirror_first)
        eigen = send(eigen, far)
        own_pair, upper_pair, *panels = call(
            pack_second,
            [blocks_shape(2), blocks_shape(2), *(blocks_shape(len(chosen)) for chosen in messages)],
            in_hbm(after(running, own), panel),
            specs=[hbm, hbm],
            scratch=[
                pltpu.VMEM((2, slab, LANES), jnp.float32),
                pltpu.VMEM((4 * slab, LANES), jnp.float32),
                pltpu.SemaphoreType.DMA((3,)),
            ],
        )
        pair_mirror = send(upper_pair, mirror_second)
        (solved,) = call(
            solve_first,
            [blocks_shape(1)],
            (after(own, *((own_pair,) if PACK_EARLY else ())), mirror, eigen, own_basis, own_values),
            flops=solve_flops,
        )

        before = send(solved, left)
        above_it = send(solved, above)
        options = {"none": (), "solved": (solved,), "before": (before,), "direct": (before, above_it)}
        panels = [
            send(after(panel_blocks, *options.get(GATE_PANEL, ())), panel_moves(chosen))
            for panel_blocks, chosen in zip(panels, messages)
        ]
        often, rarely = panels[0], panels[-1]
        ready = {"none": (), "often": (often,), "both": (often, rarely)}[GATE_SOLVE]
        (solved_next,) = call(
            solve_second,
            [blocks_shape(1)],
            (after(own_pair, *ready), upper_pair, pair_mirror, eigen, before, above_it, own_basis, own_values),
            flops=3 * solve_flops // 2,
        )
        options["next"] = (solved_next,)
        options["often"], options["both"], options["above"] = (often,), (often, rarely), (above_it,)
        options["mirror"] = (pair_mirror,)
        options["mirror_above"] = (pair_mirror, above_it)
        options["all"] = (pair_mirror, above_it, before)
        spread_first = spread(
            after(solved, *options[GATE_SPREAD]), count - 1, first, options[GATE_FORWARD], options[GATE_LOW]
        )
        pair, low_before, got, got_low = spread_first
        earlier = {"often": often, "rarely": rarely, "own": got[0], "low": low_before, "turned": got_low[0]}
        *spread_second, low = spread(solved_next, count, second, [earlier[name] for name in GATE_SECOND])
        pair_next, got_next = spread_second
        own_second = (pair_next, *got_next)
        running = update(running, panel, (pair, *got), own_second, panels)
        running = finish(running, panel, (low_before, *got_low), own_second, low, panels)
        return running.reshape(state.shape)

    placed = (
        P(None, "row", None, None, "col", None),
        P(None, "row", None, None, "col", None),
        P(None, "row", None, None),
        P(None, "row", None),
    )
    return jax.shard_map(
        local,
        mesh=mesh,
        in_specs=placed,
        out_specs=P(None, "row", None, None, "col", None),
        check_vma=False,
    )
```
